512 devices in a mesh: mx: 32 (over y, x, core), my: 16 (over z).
Axes of the slice: x: 4, y: 4, z: 16, core: 2. Of those that a mesh axis runs over, the one named last changes fastest.
Arguments:
- block: float32 [32, 655360], P(None, ('mx', 'my')), may hold values from -6 to 6
- potential: float32 [655360], P(('mx', 'my')), may hold values from -1 to 1
- cell_nodes: int32 [125, 16384], P(None, ('mx', 'my')), may hold values from 0 to 2303
- cell_scale: float32 [16384], P(('mx', 'my')), may hold values from 0.5 to 2
- stiffness: float32 [125, 125], replicated, as said below
- send_nodes: int32 [8, 65536], P(None, ('mx', 'my')), may hold values from 0 to 1279
- proj_nodes: int32 [9, 1024, 256], P(None, ('mx', 'my')), may hold values from 0 to 1279
- proj_values: float32 [9, 1024, 18, 256], P(None, ('mx', 'my')), may hold values from -0.6 to 0.6
- coupling: float32 [1024, 18], P(('mx', 'my')), may hold values from -2 to 2
Outputs:
- filtered: float32 [32, 655360], P(None, ('mx', 'my'))
The draws below stay inside these ranges and needn't reach their ends.
Inputs may be any that keep to these rules, and one draw needn't show every extreme that they name: `stiffness`: symmetric.
All inputs are finite; a program needn't handle non-finite values.
Results may differ from the reference program's by a relative error of at most 0.00015.
Values sent between devices are 32-bit elements; how exact they have to be, the bound alone decides.
A program may use at most 64 MiB of HBM per device.

```python
import math
import jax
import jax.numpy as jnp
from jax import lax

VECTORS = 32
CELL_NODES = 125
PROJECTORS = 18
DEGREES = 3
CELL_DEV = 32
SEND = 128
SUPPORT = 256
ATOM_DEV = 2
NODE_DEV = 1280
NODES = 655360
CELLS = 16384
ATOMS = 1024
SEND_ALL = 65536
N_MX = 32
N_MY = 16


def draw_stiffness(key, part):
    key = jax.random.fold_in(key, 1)
    diag_key, off_key = jax.random.split(key)
    diagonal = jax.random.uniform(diag_key, (CELL_NODES,), jnp.float32, 0.5, 1.0)
    off = jax.random.normal(off_key, (CELL_NODES, CELL_NODES), jnp.float32) * 0.03
    eye = jnp.eye(CELL_NODES, dtype=jnp.float32)
    return (off + off.T) * (1.0 - eye) + eye * diagonal[:, None]


def with_ends(drawn, rng, smallest, top_value):
    place = [jax.random.randint(jax.random.fold_in(rng, axis), (), 0, length) for axis, length in enumerate(drawn.shape)]
    widest = drawn.shape.index(max(drawn.shape))
    beside = place[:widest] + [(place[widest] + 1) % drawn.shape[widest]] + place[widest + 1:]
    return drawn.at[tuple(place)].set(smallest).at[tuple(beside)].set(top_value)


def levels(stream_key, extent, shards, smallest, largest):
    factor_of = 1.0
    for dim, shards_of in shards:
        heights = jax.random.uniform(jax.random.fold_in(jax.random.fold_in(stream_key, 6), dim), (shards_of,), jnp.float32, smallest / len(shards), largest / len(shards))
        factor_of = factor_of * jnp.repeat(jnp.exp(heights), extent[dim] // shards_of).reshape((-1,) + (1,) * (len(extent) - 1 - dim))
    return factor_of


def scatter_about(key, extent, deviation, bound, shards=(), kind=jnp.bfloat16):
    factor_of = levels(key, extent, shards, -0.22, 0.18) if shards else 1.0
    drawn = jax.random.normal(key, extent, jnp.float32) * deviation * factor_of
    return jnp.minimum(jnp.maximum(drawn, -bound), bound).astype(kind)


def setup_inputs(seed: int = 0) -> dict:
    keys = jax.random.split(jax.random.key(seed), 10)
    block = scatter_about(keys[0], (VECTORS, NODES), 1.0, 6.0, ((1, 512),), jnp.float32)
    potential = jnp.clip(jax.random.uniform(keys[1], (NODES,), jnp.float32, -1.0, 1.0) * levels(keys[1], (NODES,), ((0, 512),), -0.4, 0.0), -1.0, 1.0)
    cell_nodes = with_ends(jax.random.randint(keys[2], (CELL_NODES, CELLS), 0, NODE_DEV + 8 * SEND), jax.random.fold_in(keys[2], 1), 0, (NODE_DEV + 8 * SEND) - 1).astype(jnp.int32)
    cell_scale = jnp.clip(jnp.exp(math.log(2.0) - 1.3862944 * jax.random.uniform(keys[3], (CELLS,), jnp.float32) ** levels(keys[3], (CELLS,), ((0, 512),), -0.2, 0.2)), 0.5, 2.0)
    stiffness = draw_stiffness(jax.random.fold_in(keys[9], 71), 0)
    send_nodes = with_ends(jax.random.randint(keys[5], (8, SEND_ALL), 0, NODE_DEV), jax.random.fold_in(keys[5], 1), 0, NODE_DEV - 1).astype(jnp.int32)
    proj_nodes = with_ends(jax.random.randint(keys[6], (9, ATOMS, SUPPORT), 0, NODE_DEV), jax.random.fold_in(keys[6], 1), 0, NODE_DEV - 1).astype(jnp.int32)
    proj_values = scatter_about(keys[7], (9, ATOMS, PROJECTORS, SUPPORT), 0.1, 0.6, ((1, 512),), jnp.float32)
    coupling = jnp.clip(jax.random.uniform(keys[8], (ATOMS, PROJECTORS), jnp.float32, -2.0, 2.0) * levels(keys[8], (ATOMS, PROJECTORS), ((0, 512),), -0.4, 0.0), -2.0, 2.0)
    return {"block": block, "potential": potential, "cell_nodes": cell_nodes, "cell_scale": cell_scale, "stiffness": stiffness, "send_nodes": send_nodes, "proj_nodes": proj_nodes, "proj_values": proj_values, "coupling": coupling}


cheb_center = 5.0
cheb_half = 6.0


def with_center(eight):
    zeros = jnp.zeros_like(eight[:1])
    joined = jnp.concatenate([eight[:4], zeros, eight[4:]], axis=0)
    return joined.reshape((3, 3) + eight.shape[1:])


def without_center(nine):
    flat = nine.reshape((9,) + nine.shape[2:])
    return jnp.concatenate([flat[:4], flat[5:]], axis=0)


def flipped(pack):
    return pack[::-1, ::-1]


def neighbours(pack):
    rest = pack.shape[3:]
    grid_pack = pack.reshape((3, 3, N_MX, N_MY) + rest)
    rows_out = []
    for row_index in range(3):
        cols_out = []
        for col_index in range(3):
            cols_out.append(jnp.roll(grid_pack[row_index, col_index], (row_index - 1, col_index - 1), axis=(0, 1)))
        rows_out.append(jnp.stack(cols_out))
    return jnp.stack(rows_out).reshape(pack.shape)


def take_cols(field, indices):
    return field[:, indices]


def reference(block, potential, cell_nodes, cell_scale, stiffness, send_nodes, proj_nodes, proj_values, coupling):
    count = N_MX * N_MY
    maps = cell_nodes.reshape(CELL_NODES, count, CELL_DEV).transpose(1, 0, 2)
    scales = cell_scale.reshape(count, CELL_DEV)
    sends = send_nodes.reshape(8, count, SEND).transpose(1, 0, 2)
    pnodes = proj_nodes.reshape(9, count, ATOM_DEV, SUPPORT).transpose(1, 0, 2, 3)
    pvalues = proj_values.reshape(9, count, ATOM_DEV, PROJECTORS, SUPPORT)
    couple = coupling.reshape(count, ATOM_DEV, PROJECTORS)
    local_pot = potential.reshape(count, 1, NODE_DEV)

    def cell_work(packed):
        extended, mapping, scaling = packed
        cellv = extended[:, mapping]
        product = jnp.einsum('pq,vqc->vpc', stiffness, cellv, precision=lax.Precision.HIGHEST) * scaling
        return jnp.zeros_like(extended).at[:, mapping].add(product)

    def apply(field):
        values = jax.vmap(take_cols)(field, sends).transpose(2, 0, 1, 3)
        ghost_pack = neighbours(with_center(values))
        ghosts = without_center(ghost_pack).transpose(1, 2, 0, 3).reshape(count, VECTORS, 8 * SEND)
        extended = jnp.concatenate([field, ghosts], axis=2)
        assembled = lax.map(cell_work, (extended, maps, scales))
        own = assembled[:, :, :NODE_DEV]
        contrib = assembled[:, :, NODE_DEV:].reshape(count, VECTORS, 8, SEND).transpose(2, 0, 1, 3)
        back = without_center(flipped(neighbours(flipped(with_center(contrib)))))
        own = jax.vmap(lambda base, index, extra: base.at[:, index].add(extra))(own, sends, back.transpose(1, 2, 0, 3))
        gathered = jax.vmap(take_cols)(field, pnodes)
        partial_value = jnp.einsum('kdaps,dvkas->kdapv', pvalues, gathered, precision=lax.Precision.HIGHEST)
        arrived = neighbours(partial_value.reshape((3, 3) + partial_value.shape[1:]))
        scaled = couple[..., None] * jnp.sum(arrived, axis=(0, 1))
        spread = jnp.broadcast_to(scaled, (3, 3) + scaled.shape)
        coef = flipped(neighbours(spread)).reshape((9,) + scaled.shape)
        added = jnp.einsum('kdaps,kdapv->dvkas', pvalues, coef, precision=lax.Precision.HIGHEST)
        own = jax.vmap(lambda base, index, extra: base.at[:, index].add(extra))(own, pnodes, added)
        return own + local_pot * field

    start = block.reshape(VECTORS, count, NODE_DEV).transpose(1, 0, 2)
    previous = start
    current = (apply(start) - cheb_center * start) / cheb_half
    for degree in range(DEGREES - 1):
        following = 2.0 * (apply(current) - cheb_center * current) / cheb_half - previous
        previous = current
        current = following
    return current.transpose(1, 0, 2).reshape(VECTORS, NODES)
```

```python
import functools

import jax
import jax.numpy as jnp
from jax import lax
from jax.experimental import pallas as pl
from jax.experimental.pallas import tpu as pltpu
from jax.sharding import PartitionSpec as P

DEGREES = 3
CHEB_CENTER = 5.0
CHEB_HALF = 6.0
MESH = pl.DeviceIdType.MESH
OFFS = ((-1, -1), (-1, 0), (-1, 1), (0, -1), (0, 1), (1, -1), (1, 0), (1, 1))

VEC = 32
NODE = 1280
OWN = 5
GHO = 4
LO = 256
CN = 125
CELLS = 32
SLOTS = CELLS * 128
SENDS = 1024
PRO = 18
PPAD = 24
PK = 2 * PPAD
PALL = 9 * PK
BF = jnp.bfloat16
F32 = jnp.float32


def split(x):
    hi = x.astype(BF)
    return hi, (x - hi.astype(F32)).astype(BF)


def dot(a, b):
    return jnp.dot(a, b, preferred_element_type=F32)


def dot_nt(a, b):
    return lax.dot_general(a, b, (((1,), (1,)), ((), ())), preferred_element_type=F32)


def lanes(j, width):
    return pl.ds(pl.multiple_of(j * width, width), width)


def kernel(
    nx, ny,
    block, pot, cnodes, stiff, sends, pnodes, pvals, coup, cscale,
    out,
    field, prev, own, cellown, flhs, glhs, klhs, slhs, blhs, eall,
    ci, ct, ohg, hi8, mb, ohs, ohsend, shi8, smb, ohb, wf, whi, wlo, kmat, crow, cslab,
    sva, rva, svb, rvb,
    sema, sema_r, semb, semb_r,
):
    ix = lax.axis_index("mx")
    iy = lax.axis_index("my")

    def at(ox, oy):
        return (lax.rem(ix + ox + nx, nx), lax.rem(iy + oy + ny, ny))

    barrier = pltpu.get_barrier_semaphore()
    for ox, oy in OFFS:
        pl.semaphore_signal(barrier, inc=1, device_id=at(ox, oy), device_id_type=MESH)

    ci[...] = jnp.full((128, 128), -1, jnp.int32)
    ci[0:CN, 0:CELLS] = cnodes[...]
    ct[...] = ci[...].T
    sub = lax.broadcasted_iota(jnp.int32, (LO, 128), 0)

    def cell_tables(c, carry):
        at_c = lanes(c, 128)
        row = ct[pl.ds(c, 1), :]
        hot = jnp.where(sub == (row & (LO - 1)), 1.0, 0.0).astype(BF)
        ohg[0:LO, at_c] = hot
        ohg[LO:2 * LO, at_c] = hot
        high = jnp.broadcast_to(row >> 8, (16, 128))
        hi8[:, at_c] = high[0:8]
        for th in range(OWN + GHO):
            mb[th, :, at_c] = jnp.where(high == th, 1.0, 0.0).astype(BF)
        return carry

    lax.fori_loop(0, CELLS, cell_tables, 0)

    for k in range(8):
        at_k = slice(k * 128, (k + 1) * 128)
        row = sends[k:k + 1, :]
        hot = jnp.where(sub == (row & (LO - 1)), 1.0, 0.0).astype(BF)
        ohsend[0:LO, at_k] = hot
        ohsend[LO:2 * LO, at_k] = hot
        high = jnp.broadcast_to(row >> 8, (16, 128))
        shi8[:, at_k] = high[0:8]
        for th in range(OWN):
            smb[th, :, at_k] = jnp.where(high == th, 1.0, 0.0).astype(BF)

    wf[...] = jnp.zeros_like(wf)
    sub2 = lax.broadcasted_iota(jnp.int32, (LO, LO), 0)
    for k in range(9):
        for a in range(2):
            row = pnodes[k, a:a + 1, :]
            hot = jnp.where(sub2 == (row & (LO - 1)), 1.0, 0.0).astype(BF)
            high = jnp.broadcast_to(row >> 8, (PRO, LO))
            vhi, vlo = split(pvals[k, a])
            vhi = vhi.astype(F32)
            vlo = vlo.astype(F32)
            base = (2 * k + a) * PPAD
            for th in range(OWN):
                m = high == th
                got = dot_nt(jnp.where(m, vhi, 0.0).astype(BF), hot) + dot_nt(jnp.where(m, vlo, 0.0).astype(BF), hot)
                wf[base:base + PRO, th * LO:(th + 1) * LO] = got
    for k in range(9):
        hi, lo = split(wf[k * PK:(k + 1) * PK, :])
        whi[k * PK:(k + 1) * PK, :] = hi
        wlo[k * PK:(k + 1) * PK, :] = lo

    kf = own.at[:, 0:128]
    wf[0:128, 0:128] = jnp.zeros((128, 128), F32)
    wf[0:CN, 0:CN] = stiff[...]
    khi, klo = split(wf[0:128, 0:128])
    for r in range(2):
        kmat[r * 128:(r + 1) * 128, 0:128] = khi
        kmat[r * 128:(r + 1) * 128, 128:256] = klo

    crow[...] = jnp.zeros_like(crow)
    for h in range(2):
        for a in range(2):
            start = 64 * h + PPAD * a
            crow[0:1, start:start + PRO] = coup[a:a + 1, :]
    for m in range(DEGREES):
        for k in range(8):
            sva[m, k, VEC:VEC + 16, :] = jnp.zeros((16, 128), F32)
    cslab[...] = jnp.zeros_like(cslab)

    field[...] = block[...]
    prev[...] = jnp.zeros_like(prev)

    def apply(m, carry):
        f = field[...]
        for th in range(OWN):
            hi, lo = split(f[:, th * LO:(th + 1) * LO])
            flhs[th * VEC:(th + 1) * VEC, 0:LO] = hi
            flhs[th * VEC:(th + 1) * VEC, LO:2 * LO] = lo

        for j in range(4):
            at_j = slice(j * LO, (j + 1) * LO)
            got = dot(flhs[...], ohsend[:, at_j])
            high = shi8[0:1, at_j]
            acc = got[0:VEC]
            for th in range(1, OWN):
                acc = jnp.where(high == th, got[th * VEC:(th + 1) * VEC], acc)
            sva[m, 2 * j, 0:VEC, :] = acc[:, 0:128]
            sva[m, 2 * j + 1, 0:VEC, :] = acc[:, 128:256]
        fhi, flo = split(f)
        c = dot_nt(fhi, whi[...]) + dot_nt(flo, whi[...]) + dot_nt(fhi, wlo[...])
        for k in range(9):
            piece = c[:, k * PK:(k + 1) * PK]
            if k == 4:
                cslab[:, 0:PK] = piece[0:16]
                cslab[:, 64:64 + PK] = piece[16:32]
            else:
                d = k if k < 4 else k - 1
                sva[m, d, VEC:VEC + 16, 0:PK] = piece[0:16]
                sva[m, d, VEC:VEC + 16, 64:64 + PK] = piece[16:32]

        @pl.when(m == 0)
        def _():
            pl.semaphore_wait(barrier, 8)

        def copy_a(k):
            return pltpu.make_async_remote_copy(
                src_ref=sva.at[m, k], dst_ref=rva.at[m, k],
                send_sem=sema.at[m, k], recv_sem=sema_r.at[m, k],
                device_id=at(*OFFS[k]), device_id_type=MESH,
            )

        def copy_b(k):
            return pltpu.make_async_remote_copy(
                src_ref=svb.at[m, k], dst_ref=rvb.at[m, k],
                send_sem=semb.at[m, k], recv_sem=semb_r.at[m, k],
                device_id=at(-OFFS[k][0], -OFFS[k][1]), device_id_type=MESH,
            )

        for k in range(8):
            copy_a(k).start()

        def gather_own(j, carry):
            at_j = lanes(j, LO)
            got = dot(flhs[...], ohg[:, at_j])
            high = hi8[0:1, at_j]
            acc = jnp.where(high == 0, got[0:VEC], 0.0)
            for th in range(1, OWN):
                acc = jnp.where(high == th, got[th * VEC:(th + 1) * VEC], acc)
            cellown[:, at_j] = acc
            return carry

        lax.fori_loop(0, SLOTS // LO, gather_own, 0)

        for k in range(8):
            copy_a(k).wait_recv()
        for k in range(8):
            hi, lo = split(rva[m, k, 0:VEC, :])
            t, h = k // 2, (k % 2) * 128
            glhs[t * VEC:(t + 1) * VEC, h:h + 128] = hi
            glhs[t * VEC:(t + 1) * VEC, LO + h:LO + h + 128] = lo

        def gather_ghost(j, carry):
            at_j = lanes(j, LO)
            got = dot(glhs[...], ohg[:, at_j])
            high = hi8[0:1, at_j]
            acc = cellown[:, at_j]
            for th in range(GHO):
                acc = jnp.where(high == OWN + th, got[th * VEC:(th + 1) * VEC], acc)
            hi, lo = split(acc)
            for h in range(2):
                rows = pl.ds(pl.multiple_of(j * 2 * VEC, 2 * VEC) + h * VEC, VEC)
                klhs[rows, 0:128] = hi[:, h * 128:(h + 1) * 128]
                klhs[rows, 128:256] = lo[:, h * 128:(h + 1) * 128]
            return carry

        lax.fori_loop(0, SLOTS // LO, gather_ghost, 0)

        def products(j, carry):
            got = dot(klhs[lanes(j, 256), :], kmat[...])
            prod = got[:, 0:128] + got[:, 128:256]
            for i in range(8):
                at_c = pl.ds(pl.multiple_of(j * 1024, 1024) + i * 128, 128)
                hi, lo = split(prod[i * VEC:(i + 1) * VEC] * cscale[j * 8 + i])
                for th in range(OWN + GHO):
                    mask = mb[th, :, at_c]
                    base = th * 2 * VEC
                    for r in range(2):
                        slhs[base + 16 * r:base + 16 * r + 16, at_c] = hi[16 * r:16 * r + 16] * mask
                        slhs[base + VEC + 16 * r:base + VEC + 16 * r + 16, at_c] = lo[16 * r:16 * r + 16] * mask
            return carry

        lax.fori_loop(0, CELLS // 8, products, 0)

        got = dot_nt(slhs[OWN * 2 * VEC:(OWN + GHO) * 2 * VEC, :], ohg[0:LO, :])
        for t in range(GHO):
            both = got[t * 2 * VEC:t * 2 * VEC + VEC] + got[t * 2 * VEC + VEC:(t + 1) * 2 * VEC]
            svb[m, 2 * t, 0:VEC, :] = both[:, 0:128]
            svb[m, 2 * t + 1, 0:VEC, :] = both[:, 128:256]
        total = cslab[...]
        for k in range(8):
            total = total + rva[m, k, VEC:VEC + 16, :]
        coef = total * crow[0:1, :]
        for k in range(8):
            svb[m, k, VEC:VEC + 16, :] = coef
            copy_b(k).start()

        f = field[...]
        got = dot_nt(slhs[0:OWN * 2 * VEC, :], ohg[0:LO, :])
        base = (pot[...] - CHEB_CENTER) * f
        for th in range(OWN):
            at_t = slice(th * LO, (th + 1) * LO)
            both = got[th * 2 * VEC:th * 2 * VEC + VEC] + got[th * 2 * VEC + VEC:(th + 1) * 2 * VEC]
            own[:, at_t] = both + base[:, at_t]

        for k in range(8):
            copy_b(k).wait_recv()
        for k in range(8):
            at_k = slice(k * 128, (k + 1) * 128)
            hi, lo = split(rvb[m, k, 0:VEC, :])
            for th in range(OWN):
                mask = smb[th, :, at_k]
                row = th * 2 * VEC
                for r in range(2):
                    blhs[row + 16 * r:row + 16 * r + 16, at_k] = hi[16 * r:16 * r + 16] * mask
                    blhs[row + VEC + 16 * r:row + VEC + 16 * r + 16, at_k] = lo[16 * r:16 * r + 16] * mask
        for k in range(9):
            if k == 4:
                slab = coef
            else:
                slab = rvb[m, k if k < 4 else k - 1, VEC:VEC + 16, :]
            eall[0:16, k * PK:(k + 1) * PK] = slab[:, 0:PK]
            eall[16:32, k * PK:(k + 1) * PK] = slab[:, 64:64 + PK]
        ehi, elo = split(eall[...])
        spread = dot(ehi, whi[...]) + dot(elo, whi[...]) + dot(ehi, wlo[...])
        got = dot_nt(blhs[...], ohsend[0:LO, :])
        alpha = jnp.where(m == 0, 1.0 / CHEB_HALF, 2.0 / CHEB_HALF)
        for th in range(OWN):
            at_t = slice(th * LO, (th + 1) * LO)
            both = got[th * 2 * VEC:th * 2 * VEC + VEC] + got[th * 2 * VEC + VEC:(th + 1) * 2 * VEC]
            new = alpha * (own[:, at_t] + both + spread[:, at_t]) - prev[:, at_t]
            prev[:, at_t] = field[:, at_t]
            field[:, at_t] = new
        for k in range(8):
            copy_a(k).wait_send()
            copy_b(k).wait_send()
        return carry

    lax.fori_loop(0, DEGREES, apply, 0)
    out[...] = field[...]


def shards(block, potential, cell_nodes, cell_scale, stiffness, send_nodes, proj_nodes, proj_values, coupling):
    nx, ny = lax.axis_size("mx"), lax.axis_size("my")
    vmem = pl.BlockSpec(memory_space=pltpu.VMEM)
    smem = pl.BlockSpec(memory_space=pltpu.SMEM)
    msg = pltpu.VMEM((DEGREES, 8, VEC + 16, 128), F32)
    sem = pltpu.SemaphoreType.DMA((DEGREES, 8))
    return pl.pallas_call(
        functools.partial(kernel, nx, ny),
        out_shape=jax.ShapeDtypeStruct((VEC, NODE), F32),
        in_specs=[vmem] * 8 + [smem],
        out_specs=vmem,
        scratch_shapes=[
            pltpu.VMEM((VEC, NODE), F32),
            pltpu.VMEM((VEC, NODE), F32),
            pltpu.VMEM((VEC, NODE), F32),
            pltpu.VMEM((VEC, SLOTS), F32),
            pltpu.VMEM((OWN * VEC, 2 * LO), BF),
            pltpu.VMEM((GHO * VEC, 2 * LO), BF),
            pltpu.VMEM((CELLS * VEC, 256), BF),
            pltpu.VMEM(((OWN + GHO) * 2 * VEC, SLOTS), BF),
            pltpu.VMEM((OWN * 2 * VEC, SENDS), BF),
            pltpu.VMEM((VEC, PALL), F32),
            pltpu.VMEM((128, 128), jnp.int32),
            pltpu.VMEM((128, 128), jnp.int32),
            pltpu.VMEM((2 * LO, SLOTS), BF),
            pltpu.VMEM((8, SLOTS), jnp.int32),
            pltpu.VMEM((OWN + GHO, 16, SLOTS), BF),
            pltpu.VMEM((16, 128), BF),
            pltpu.VMEM((2 * LO, SENDS), BF),
            pltpu.VMEM((8, SENDS), jnp.int32),
            pltpu.VMEM((OWN, 16, SENDS), BF),
            pltpu.VMEM((16, 128), BF),
            pltpu.VMEM((PALL, NODE), F32),
            pltpu.VMEM((PALL, NODE), BF),
            pltpu.VMEM((PALL, NODE), BF),
            pltpu.VMEM((256, 256), BF),
            pltpu.VMEM((8, 128), F32),
            pltpu.VMEM((16, 128), F32),
            msg, msg, msg, msg,
            sem, sem, sem, sem,
        ],
        compiler_params=pltpu.CompilerParams(
            collective_id=0, has_side_effects=True, vmem_limit_bytes=48 * 1024 * 1024
        ),
        name="filtered",
    )(block, potential.reshape(1, NODE), cell_nodes, stiffness, send_nodes, proj_nodes, proj_values, coupling, cell_scale)


def solution(mesh):
    both = ("mx", "my")
    placed = (
        P(None, both), P(both), P(None, both), P(both), P(), P(None, both),
        P(None, both, None), P(None, both, None, None), P(both, None),
    )
    return jax.shard_map(shards, mesh=mesh, in_specs=placed, out_specs=P(None, both), check_vma=False)
```

```python
import functools

import jax
import jax.numpy as jnp
from jax import lax
from jax.experimental import pallas as pl
from jax.experimental.pallas import tpu as pltpu
from jax.sharding import PartitionSpec as P

DEGREES = 3
CHEB_CENTER = 5.0
CHEB_HALF = 6.0
MESH = pl.DeviceIdType.MESH
OFFS = ((-1, -1), (-1, 0), (-1, 1), (0, -1), (0, 1), (1, -1), (1, 0), (1, 1))
DIAGONAL_FIRST = (0, 2, 5, 7, 1, 6, 3, 4)

VEC = 32
NODE = 1280
OWN = 5
GHO = 4
LO = 256
CN = 125
CELLS = 32
SLOTS = CELLS * 128
SENDS = 1024
PRO = 18
PPAD = 24
PK = 2 * PPAD
PALL = 9 * PK
BF = jnp.bfloat16
F32 = jnp.float32


def split(x):
    hi = x.astype(BF)
    return hi, (x - hi.astype(F32)).astype(BF)


def both(x):
    hi, lo = split(x)
    return jnp.concatenate([hi, lo], axis=0)


def dot(a, b):
    return jnp.dot(a, b, preferred_element_type=F32)


def dot_nt(a, b):
    return lax.dot_general(a, b, (((1,), (1,)), ((), ())), preferred_element_type=F32)


def block_of(got, th):
    row = th * 2 * VEC
    return got[row:row + VEC] + got[row + VEC:row + 2 * VEC]


def picked(got, high, first, count, acc):
    for th in range(count):
        one = block_of(got, th)
        acc = one if acc is None else jnp.where(high == first + th, one, acc)
    return acc


def hot_rows(row, iota):
    return jnp.where(iota == (row & (LO - 1)), 1.0, 0.0).astype(BF)


def kernel(
    nx, ny,
    block, pot, cnodes, stiff, sends, pnodes, pvals, coup, cscale,
    out,
    field, prev, own, cellown, flhs, glhs, klhs, slhs, blhs, eall,
    ct, ohg, hi8, mb, ohsend, shi8, smb, whi, wlo, kf, kmat, crow, cslab,
    sva, rva, svb, rvb, svc, rvc, sve, rve,
    sema, sema_r, semb, semb_r, semc, semc_r, seme, seme_r,
):
    ix = lax.axis_index("mx")
    iy = lax.axis_index("my")

    def at(ox, oy):
        return (lax.rem(ix + ox + nx, nx), lax.rem(iy + oy + ny, ny))

    if REMOTE:
        barrier = pltpu.get_barrier_semaphore()
        for ox, oy in OFFS:
            pl.semaphore_signal(barrier, inc=1, device_id=at(ox, oy), device_id_type=MESH)

    sub = lax.broadcasted_iota(jnp.int32, (LO, 128), 0)
    for k in range(8):
        at_k = slice(k * 128, (k + 1) * 128)
        row = sends[k:k + 1, :]
        ohsend[:, at_k] = hot_rows(row, sub)
        high = jnp.broadcast_to(row >> 8, (16, 128))
        shi8[:, at_k] = high[0:8]
        for th in range(OWN):
            smb[th, :, at_k] = jnp.where(high == th, 1.0, 0.0).astype(BF)

    ct[...] = jnp.full((CELLS, 128), -1, jnp.int32)
    ct[:, 0:CN] = cnodes[...]
    for c in range(CELLS):
        at_c = slice(c * 128, (c + 1) * 128)
        row = ct[c:c + 1, :]
        ohg[:, at_c] = hot_rows(row, sub)
        high = jnp.broadcast_to(row >> 8, (16, 128))
        hi8[:, at_c] = high[0:8]
        for th in range(OWN + GHO):
            mb[th, :, at_c] = jnp.where(high == th, 1.0, 0.0).astype(BF)

    sub2 = lax.broadcasted_iota(jnp.int32, (LO, LO), 0)
    pad = jnp.zeros((PPAD - PRO, LO), F32)
    for k in range(9):
        parts = []
        for a in range(2):
            row = pnodes[k, a:a + 1, :]
            high = jnp.broadcast_to(row >> 8, (16, LO))
            v = jnp.concatenate([pvals[k, :, a, :], pad], axis=0)
            vhi = v.astype(BF).astype(F32)
            v2 = jnp.concatenate([vhi, v - vhi], axis=0).astype(BF)
            rows = []
            for th in range(OWN):
                mask = jnp.where(high == th, 1.0, 0.0).astype(BF)
                rows.append(v2 * jnp.concatenate([mask] * 3, axis=0))
            got = dot_nt(jnp.concatenate(rows, axis=0), hot_rows(row, sub2))
            parts.append([got[th * PK:th * PK + PPAD] + got[th * PK + PPAD:(th + 1) * PK] for th in range(OWN)])
        for th in range(OWN):
            hi, lo = split(jnp.concatenate([parts[0][th], parts[1][th]], axis=0))
            whi[k * PK:(k + 1) * PK, th * LO:(th + 1) * LO] = hi
            wlo[k * PK:(k + 1) * PK, th * LO:(th + 1) * LO] = lo

    kf[...] = jnp.zeros((128, 128), F32)
    kf[0:CN, 0:CN] = stiff[...]
    khi, klo = split(kf[...])
    for r in range(2):
        kmat[r * 128:(r + 1) * 128, 0:128] = khi
        kmat[r * 128:(r + 1) * 128, 128:256] = klo

    crow[...] = jnp.zeros_like(crow)
    for h in range(2):
        for a in range(2):
            start = 64 * h + PPAD * a
            crow[0:1, start:start + PRO] = coup[a:a + 1, :]
    for m in range(DEGREES):
        for k in range(8):
            svc[m, k] = jnp.zeros((16, 128), F32)
    cslab[...] = jnp.zeros_like(cslab)

    field[...] = block[...]
    prev[...] = jnp.zeros_like(prev)

    def apply(m, carry):
        def copies(src, dst, send, recv, sign):
            return [
                pltpu.make_async_remote_copy(
                    src_ref=src.at[m, k], dst_ref=dst.at[m, k], send_sem=send.at[m, k], recv_sem=recv.at[m, k],
                    device_id=at(sign * OFFS[k][0], sign * OFFS[k][1]), device_id_type=MESH,
                )
                for k in range(8)
            ]

        ghosts = copies(sva, rva, sema, sema_r, 1)
        sums = copies(svc, rvc, semc, semc_r, 1)
        backs = copies(svb, rvb, semb, semb_r, -1)
        coefs = copies(sve, rve, seme, seme_r, -1)

        def start(group):
            if REMOTE:
                for k in DIAGONAL_FIRST:
                    group[k].start()

        def arrive(group):
            if REMOTE:
                for k in DIAGONAL_FIRST[::-1]:
                    group[k].wait_recv()

        f = field[...]
        for th in range(OWN):
            flhs[th * 2 * VEC:(th + 1) * 2 * VEC, :] = both(f[:, th * LO:(th + 1) * LO])

        for j in range(4):
            at_j = slice(j * LO, (j + 1) * LO)
            acc = picked(dot(flhs[...], ohsend[:, at_j]), shi8[0:1, at_j], 0, OWN, None)
            sva[m, 2 * j] = acc[:, 0:128]
            sva[m, 2 * j + 1] = acc[:, 128:256]

        if REMOTE:
            @pl.when(m == 0)
            def _():
                pl.semaphore_wait(barrier, 8)

        start(ghosts)

        f2 = both(f)
        c2 = dot_nt(f2, whi[...])
        c = c2[0:VEC] + c2[VEC:2 * VEC] + dot_nt(f2[0:VEC], wlo[...])
        for k in range(9):
            piece = c[:, k * PK:(k + 1) * PK]
            if k == 4:
                cslab[:, 0:PK] = piece[0:16]
                cslab[:, 64:64 + PK] = piece[16:32]
            else:
                d = k if k < 4 else k - 1
                svc[m, d, :, 0:PK] = piece[0:16]
                svc[m, d, :, 64:64 + PK] = piece[16:32]
        start(sums)

        for j in range(SLOTS // LO):
            at_j = slice(j * LO, (j + 1) * LO)
            cellown[:, at_j] = picked(dot(flhs[...], ohg[:, at_j]), hi8[0:1, at_j], 0, OWN, None)

        arrive(ghosts)
        for t in range(GHO):
            glhs[t * 2 * VEC:(t + 1) * 2 * VEC, 0:128] = both(rva[m, 2 * t])
            glhs[t * 2 * VEC:(t + 1) * 2 * VEC, 128:256] = both(rva[m, 2 * t + 1])
        for j in range(SLOTS // LO):
            at_j = slice(j * LO, (j + 1) * LO)
            high = hi8[0:1, at_j]
            acc = jnp.where(high >= 0, cellown[:, at_j], 0.0)
            acc = picked(dot(glhs[...], ohg[:, at_j]), high, OWN, GHO, acc)
            hi, lo = split(acc)
            for h in range(2):
                rows = slice((2 * j + h) * VEC, (2 * j + h + 1) * VEC)
                klhs[rows, 0:128] = hi[:, h * 128:(h + 1) * 128]
                klhs[rows, 128:256] = lo[:, h * 128:(h + 1) * 128]

        for j in range(CELLS // 8):
            got = dot(klhs[j * 256:(j + 1) * 256, :], kmat[...])
            prod = got[:, 0:128] + got[:, 128:256]
            for i in range(8):
                c0 = j * 8 + i
                at_c = slice(c0 * 128, (c0 + 1) * 128)
                pair = both(prod[i * VEC:(i + 1) * VEC] * cscale[c0])
                for th in range(OWN + GHO):
                    mask = jnp.concatenate([mb[th, :, at_c]] * 4, axis=0)
                    slhs[th * 2 * VEC:(th + 1) * 2 * VEC, at_c] = pair * mask

        arrive(sums)
        total = cslab[...]
        for k in range(8):
            total = total + (rvc if REMOTE else svc)[m, k]
        coef = total * crow[0:1, :]
        for k in range(8):
            sve[m, k] = coef
        start(coefs)

        got = dot_nt(slhs[OWN * 2 * VEC:(OWN + GHO) * 2 * VEC, :], ohg[...])
        for t in range(GHO):
            one = block_of(got, t)
            svb[m, 2 * t] = one[:, 0:128]
            svb[m, 2 * t + 1] = one[:, 128:256]
        start(backs)

        got = dot_nt(slhs[0:OWN * 2 * VEC, :], ohg[...])
        base = (pot[...] - CHEB_CENTER) * field[...]
        arrive(coefs)
        for k in range(9):
            slab = coef if k == 4 else (rve if REMOTE else sve)[m, k if k < 4 else k - 1]
            eall[0:16, k * PK:(k + 1) * PK] = slab[:, 0:PK]
            eall[16:32, k * PK:(k + 1) * PK] = slab[:, 64:64 + PK]
        e2 = both(eall[...])
        s2 = dot(e2, whi[...])
        base = base + (s2[0:VEC] + s2[VEC:2 * VEC] + dot(e2[0:VEC], wlo[...]))
        for th in range(OWN):
            at_t = slice(th * LO, (th + 1) * LO)
            own[:, at_t] = block_of(got, th) + base[:, at_t]

        arrive(backs)
        for k in range(8):
            at_k = slice(k * 128, (k + 1) * 128)
            pair = both((rvb if REMOTE else svb)[m, k])
            for th in range(OWN):
                blhs[th * 2 * VEC:(th + 1) * 2 * VEC, at_k] = pair * jnp.concatenate([smb[th, :, at_k]] * 4, axis=0)
        got = dot_nt(blhs[...], ohsend[...])
        alpha = jnp.where(m == 0, 1.0 / CHEB_HALF, 2.0 / CHEB_HALF)
        for th in range(OWN):
            at_t = slice(th * LO, (th + 1) * LO)
            new = alpha * (own[:, at_t] + block_of(got, th)) - prev[:, at_t]
            prev[:, at_t] = field[:, at_t]
            field[:, at_t] = new
        if REMOTE:
            for group in (ghosts, sums, backs, coefs):
                for one in group:
                    one.wait_send()
        return carry

    lax.fori_loop(0, DEGREES, apply, 0)
    out[...] = field[...]


REMOTE = True


def shards(block, potential, cell_nodes, cell_scale, stiffness, send_nodes, proj_nodes, proj_values, coupling):
    nx, ny = lax.axis_size("mx"), lax.axis_size("my")
    vmem = pl.BlockSpec(memory_space=pltpu.VMEM)
    smem = pl.BlockSpec(memory_space=pltpu.SMEM)
    halo = pltpu.VMEM((DEGREES, 8, VEC, 128), F32)
    slab = pltpu.VMEM((DEGREES, 8, 16, 128), F32)
    sem = pltpu.SemaphoreType.DMA((DEGREES, 8))
    return pl.pallas_call(
        functools.partial(kernel, nx, ny),
        out_shape=jax.ShapeDtypeStruct((VEC, NODE), F32),
        in_specs=[vmem] * 8 + [smem],
        out_specs=vmem,
        scratch_shapes=[
            pltpu.VMEM((VEC, NODE), F32),
            pltpu.VMEM((VEC, NODE), F32),
            pltpu.VMEM((VEC, NODE), F32),
            pltpu.VMEM((VEC, SLOTS), F32),
            pltpu.VMEM((OWN * 2 * VEC, LO), BF),
            pltpu.VMEM((GHO * 2 * VEC, LO), BF),
            pltpu.VMEM((CELLS * VEC, 256), BF),
            pltpu.VMEM(((OWN + GHO) * 2 * VEC, SLOTS), BF),
            pltpu.VMEM((OWN * 2 * VEC, SENDS), BF),
            pltpu.VMEM((VEC, PALL), F32),
            pltpu.VMEM((CELLS, 128), jnp.int32),
            pltpu.VMEM((LO, SLOTS), BF),
            pltpu.VMEM((8, SLOTS), jnp.int32),
            pltpu.VMEM((OWN + GHO, 16, SLOTS), BF),
            pltpu.VMEM((LO, SENDS), BF),
            pltpu.VMEM((8, SENDS), jnp.int32),
            pltpu.VMEM((OWN, 16, SENDS), BF),
            pltpu.VMEM((PALL, NODE), BF),
            pltpu.VMEM((PALL, NODE), BF),
            pltpu.VMEM((128, 128), F32),
            pltpu.VMEM((256, 256), BF),
            pltpu.VMEM((8, 128), F32),
            pltpu.VMEM((16, 128), F32),
            halo, halo, halo, halo, slab, slab, slab, slab,
            sem, sem, sem, sem, sem, sem, sem, sem,
        ],
        compiler_params=pltpu.CompilerParams(
            collective_id=0, has_side_effects=True, vmem_limit_bytes=48 * 1024 * 1024
        ) if REMOTE else pltpu.CompilerParams(has_side_effects=True, vmem_limit_bytes=48 * 1024 * 1024),
        name="filtered",
    )(
        block, potential.reshape(1, NODE), cell_nodes.T, stiffness, send_nodes, proj_nodes,
        proj_values.transpose(0, 2, 1, 3), coupling, cell_scale,
    )


def solution(mesh):
    axes = ("mx", "my")
    placed = (
        P(None, axes), P(axes), P(None, axes), P(axes), P(), P(None, axes),
        P(None, axes, None), P(None, axes, None, None), P(axes, None),
    )
    return jax.shard_map(shards, mesh=mesh, in_specs=placed, out_specs=P(None, axes), check_vma=False)
```

```python
import functools

import jax
import jax.numpy as jnp
from jax import lax
from jax.experimental import pallas as pl
from jax.experimental.pallas import tpu as pltpu
from jax.sharding import PartitionSpec as P

DEGREES = 3
CHEB_CENTER = 5.0
CHEB_HALF = 6.0
MESH = pl.DeviceIdType.MESH
OFFS = ((-1, -1), (-1, 0), (-1, 1), (0, -1), (0, 1), (1, -1), (1, 0), (1, 1))
CARD, DIAG = (1, 6, 3, 4), (0, 2, 5, 7)
ORDER = CARD + DIAG

VEC = 32
NODE = 1280
OWN = 5
GHO = 4
LO = 256
CN = 125
CELLS = 32
SLOTS = CELLS * 128
SENDS = 1024
PRO = 18
PPAD = 24
PK = 2 * PPAD
PALL = 9 * PK
BF = jnp.bfloat16
F32 = jnp.float32


def split(x):
    hi = x.astype(BF)
    return hi, (x - hi.astype(F32)).astype(BF)


def both(x):
    hi, lo = split(x)
    return jnp.concatenate([hi, lo], axis=0)


def dot(a, b):
    return jnp.dot(a, b, preferred_element_type=F32)


def dot_nt(a, b):
    return lax.dot_general(a, b, (((1,), (1,)), ((), ())), preferred_element_type=F32)


def block_of(got, th):
    row = th * 2 * VEC
    return got[row:row + VEC] + got[row + VEC:row + 2 * VEC]


def picked(got, high, first, count, acc):
    for th in range(count):
        one = block_of(got, th)
        acc = one if acc is None else jnp.where(high == first + th, one, acc)
    return acc


def hot_rows(row, iota):
    return jnp.where(iota == (row & (LO - 1)), 1.0, 0.0).astype(BF)


def kernel(
    nx, ny,
    a_block, a_pot, a_cnodes, a_stiff, a_sends, a_pnodes, a_pvals, a_coup, a_cscale,
    out,
    block, pot, cnodes, stiff, sends, pnodes, pvals, coup, cscale, insem,
    prev, own, cellown, flhs, glhs, klhs, prods, slhs, blhs, eall,
    ct, ohg, hi8, mb, ohs, ohsend, shi8, smb, ohb, wf, whi, wlo, twhi, twlo, kf, kmat, crow, cslab,
    sva, rva, svb, rvb, svc, rvc, sve, rve,
    sema, sema_r, semb, semb_r, semc, semc_r, seme, seme_r,
):
    ix = lax.axis_index("mx")
    iy = lax.axis_index("my")

    def at(ox, oy):
        return (lax.rem(ix + ox + nx, nx), lax.rem(iy + oy + ny, ny))

    if REMOTE:
        barrier = pltpu.get_barrier_semaphore()
        for k in ORDER[::-1]:
            pl.semaphore_signal(barrier, inc=1, device_id=at(*OFFS[k]), device_id_type=MESH)

    pairs = (
        (a_sends, sends), (a_block, block), (a_cnodes, cnodes), (a_pnodes, pnodes), (a_pvals, pvals),
        (a_stiff, stiff), (a_coup, coup), (a_cscale, cscale), (a_pot, pot),
    )
    loads = {id(dst): pltpu.make_async_copy(src, dst, insem.at[i]) for i, (src, dst) in enumerate(pairs)}
    for one in loads.values():
        one.start()

    def ready(*refs):
        for ref in refs:
            loads[id(ref)].wait()

    def copies(m, src, dst, send, recv, sign):
        return {
            k: pltpu.make_async_remote_copy(
                src_ref=src.at[m, k], dst_ref=dst.at[m, k], send_sem=send.at[m, k], recv_sem=recv.at[m, k],
                device_id=at(sign * OFFS[k][0], sign * OFFS[k][1]), device_id_type=MESH,
            )
            for k in range(8)
        } if REMOTE else {}

    def start(group, which):
        for k in which:
            if REMOTE:
                group[k].start()

    def arrive(group, which):
        for k in which:
            if REMOTE:
                group[k].wait_recv()

    def sent(*groups):
        for group in groups:
            for one in group.values():
                one.wait_send()

    def send_values(m, before_first):
        ghosts = copies(m, sva, rva, sema, sema_r, 1)
        for j in (2, 3, 0, 1):
            at_j = slice(j * LO, (j + 1) * LO)
            acc = picked(dot(flhs[...], ohsend[:, at_j]), shi8[0:1, at_j], 0, OWN, None)
            sva[m, ORDER[2 * j]] = acc[:, 0:128]
            sva[m, ORDER[2 * j + 1]] = acc[:, 128:256]
            if j == 3:
                before_first()
                start(ghosts, DIAG)
        start(ghosts, CARD)

    def field_rows():
        for th in range(OWN):
            flhs[th * 2 * VEC:(th + 1) * 2 * VEC, :] = both(out[:, th * LO:(th + 1) * LO])

    sub = lax.broadcasted_iota(jnp.int32, (LO, 128), 0)
    ready(sends)
    for q, k in enumerate(ORDER):
        at_q = slice(q * 128, (q + 1) * 128)
        row = sends[k:k + 1, :]
        ohsend[:, at_q] = hot_rows(row, sub)
        shi8[:, at_q] = jnp.broadcast_to(row >> 8, (8, 128))
    ready(block)
    out[...] = block[...]
    field_rows()

    def met():
        if REMOTE:
            pl.semaphore_wait(barrier, 8)

    send_values(0, met)

    ct[...] = jnp.full((128, 128), -1, jnp.int32)
    ready(cnodes)
    ct[0:CELLS, 0:CN] = cnodes[...]
    pos = ct[0:CELLS, :]
    slot = (pos >> 7) - 2 * OWN
    new = slot
    for q, k in enumerate(ORDER):
        new = jnp.where(slot == k, q, new)
    ct[0:CELLS, :] = jnp.where(slot >= 0, ((new + 2 * OWN) << 7) + (pos & 127), pos)
    for q, k in enumerate(ORDER):
        ct[CELLS + q:CELLS + q + 1, :] = sends[k:k + 1, :]
    cols = ct[...].T
    lane = lax.broadcasted_iota(jnp.int32, (128, LO), 1)
    for c in range(CELLS):
        at_c = slice(c * 128, (c + 1) * 128)
        row = ct[c:c + 1, :]
        ohg[:, at_c] = hot_rows(row, sub)
        ohs[at_c, :] = hot_rows(jnp.broadcast_to(cols[:, c:c + 1], (128, LO)), lane)
        high = jnp.broadcast_to(row >> 8, (16, 128))
        hi8[:, at_c] = high[0:8]
        for th in range(OWN + GHO):
            mb[th, :, at_c] = jnp.where(high == th, 1.0, 0.0).astype(BF)
    for q in range(8):
        at_q = slice(q * 128, (q + 1) * 128)
        high = jnp.broadcast_to(ct[CELLS + q:CELLS + q + 1, :] >> 8, (16, 128))
        ohb[at_q, :] = hot_rows(jnp.broadcast_to(cols[:, CELLS + q:CELLS + q + 1], (128, LO)), lane)
        for th in range(OWN):
            smb[th, :, at_q] = jnp.where(high == th, 1.0, 0.0).astype(BF)

    ready(pnodes, pvals)
    sub2 = lax.broadcasted_iota(jnp.int32, (LO, LO), 0)
    pad = jnp.zeros((PPAD - PRO, LO), F32)
    for k in range(9):
        parts = []
        for a in range(2):
            row = pnodes[k, a:a + 1, :]
            high = jnp.broadcast_to(row >> 8, (16, LO))
            v = jnp.concatenate([pvals[k, :, a, :], pad], axis=0)
            vhi = v.astype(BF).astype(F32)
            v2 = jnp.concatenate([vhi, v - vhi], axis=0).astype(BF)
            rows = []
            for th in range(OWN):
                mask = jnp.where(high == th, 1.0, 0.0).astype(BF)
                rows.append(v2 * jnp.concatenate([mask] * 3, axis=0))
            got = dot_nt(jnp.concatenate(rows, axis=0), hot_rows(row, sub2))
            parts.append([got[th * PK:th * PK + PPAD] + got[th * PK + PPAD:(th + 1) * PK] for th in range(OWN)])
        for th in range(OWN):
            at_t = slice(th * LO, (th + 1) * LO)
            w = jnp.concatenate([parts[0][th], parts[1][th]], axis=0)
            hi, lo = split(w)
            wf[k * PK:(k + 1) * PK, at_t] = w
            whi[k * PK:(k + 1) * PK, at_t] = hi
            wlo[k * PK:(k + 1) * PK, at_t] = lo
    wf[PALL:512, :] = jnp.zeros((512 - PALL, NODE), F32)
    for n in range(NODE // 128):
        at_n = slice(n * 128, (n + 1) * 128)
        for r in range(4):
            at_r = slice(r * 128, (r + 1) * 128)
            hi, lo = split(wf[at_r, at_n].T)
            twhi[at_n, at_r] = hi
            twlo[at_n, at_r] = lo

    ready(stiff, coup, cscale, pot)
    kf[...] = jnp.zeros((128, 128), F32)
    kf[0:CN, 0:CN] = stiff[...]
    khi, klo = split(kf[...])
    for r in range(2):
        kmat[r * 128:(r + 1) * 128, 0:128] = khi
        kmat[r * 128:(r + 1) * 128, 128:256] = klo

    crow[...] = jnp.zeros_like(crow)
    for h in range(2):
        for a in range(2):
            first = 64 * h + PPAD * a
            crow[0:1, first:first + PRO] = coup[a:a + 1, :]
    for m in range(DEGREES):
        for k in range(8):
            svc[m, k] = jnp.zeros((16, 128), F32)
    cslab[...] = jnp.zeros_like(cslab)
    prev[...] = jnp.zeros_like(prev)

    def masked(th, at_c):
        return prods[:, at_c] * jnp.concatenate([mb[th, :, at_c]] * 4, axis=0)

    def scatter_rows(first, count):
        for th in range(first, first + count):
            for c in range(SLOTS // 512):
                at_c = slice(c * 512, (c + 1) * 512)
                slhs[th * 2 * VEC:(th + 1) * 2 * VEC, at_c] = masked(th, at_c)
        return dot(slhs[first * 2 * VEC:(first + count) * 2 * VEC, :], ohs[...])

    def apply(m, carry):
        ghosts = copies(m, sva, rva, sema, sema_r, 1)
        sums = copies(m, svc, rvc, semc, semc_r, 1)
        backs = copies(m, svb, rvb, semb, semb_r, -1)
        coefs = copies(m, sve, rve, seme, seme_r, -1)

        f2 = both(out[...])
        c2 = dot(f2, twhi[...])
        c = c2[0:VEC] + c2[VEC:2 * VEC] + dot(f2[0:VEC], twlo[...])
        for k in range(9):
            piece = c[:, k * PK:(k + 1) * PK]
            if k == 4:
                cslab[:, 0:PK] = piece[0:16]
                cslab[:, 64:64 + PK] = piece[16:32]
            else:
                d = k if k < 4 else k - 1
                svc[m, d, :, 0:PK] = piece[0:16]
                svc[m, d, :, 64:64 + PK] = piece[16:32]
        start(sums, ORDER[::-1])

        for j in range(SLOTS // LO):
            at_j = slice(j * LO, (j + 1) * LO)
            acc = picked(dot(flhs[...], ohg[:, at_j]), hi8[0:1, at_j], 0, OWN, None)
            cellown[:, at_j] = jnp.where(hi8[0:1, at_j] >= 0, acc, 0.0)

        def ghost_columns(first, which, use):
            arrive(ghosts, which)
            for t in range(first, first + 2):
                glhs[t * 2 * VEC:(t + 1) * 2 * VEC, 0:128] = both((rva if REMOTE else sva)[m, ORDER[2 * t]])
                glhs[t * 2 * VEC:(t + 1) * 2 * VEC, 128:256] = both((rva if REMOTE else sva)[m, ORDER[2 * t + 1]])
            part = glhs[first * 2 * VEC:(first + 2) * 2 * VEC, :]
            for j in range(SLOTS // LO):
                at_j = slice(j * LO, (j + 1) * LO)
                use(j, at_j, picked(dot(part, ohg[:, at_j]), hi8[0:1, at_j], OWN + first, 2, cellown[:, at_j]))

        def keep(j, at_j, acc):
            cellown[:, at_j] = acc

        def stack(j, at_j, acc):
            hi, lo = split(acc)
            for h in range(2):
                rows = slice((2 * j + h) * VEC, (2 * j + h + 1) * VEC)
                klhs[rows, 0:128] = hi[:, h * 128:(h + 1) * 128]
                klhs[rows, 128:256] = lo[:, h * 128:(h + 1) * 128]

        ghost_columns(0, CARD, keep)
        ghost_columns(2, DIAG, stack)

        for j in range(CELLS // 8):
            got = dot(klhs[j * 256:(j + 1) * 256, :], kmat[...])
            prod = got[:, 0:128] + got[:, 128:256]
            for i in range(8):
                c0 = j * 8 + i
                prods[:, c0 * 128:(c0 + 1) * 128] = both(prod[i * VEC:(i + 1) * VEC] * cscale[c0])

        arrive(sums, ORDER)
        total = cslab[...]
        for k in range(8):
            total = total + (rvc if REMOTE else svc)[m, k]
        coef = total * crow[0:1, :]
        for k in range(8):
            sve[m, k] = coef
        start(coefs, ORDER[::-1])

        def give_back(first, which):
            got = scatter_rows(OWN + first, 2)
            for t in range(2):
                one = block_of(got, t)
                svb[m, ORDER[2 * (first + t)]] = one[:, 0:128]
                svb[m, ORDER[2 * (first + t) + 1]] = one[:, 128:256]
            start(backs, which)

        give_back(2, DIAG)
        give_back(0, CARD)

        got = scatter_rows(0, OWN)
        for n in range(NODE // 128):
            at_n = slice(n * 128, (n + 1) * 128)
            own[:, at_n] = (pot[n:n + 1, :] - CHEB_CENTER) * out[:, at_n]
        for th in range(OWN):
            own[:, th * LO:(th + 1) * LO] += block_of(got, th)
        sent(ghosts, sums)
        arrive(coefs, ORDER)
        for k in range(9):
            slab = coef if k == 4 else (rve if REMOTE else sve)[m, k if k < 4 else k - 1]
            eall[0:16, k * PK:(k + 1) * PK] = slab[:, 0:PK]
            eall[16:32, k * PK:(k + 1) * PK] = slab[:, 64:64 + PK]
        e2 = both(eall[...])
        s2 = dot(e2, whi[...])
        own[...] += s2[0:VEC] + s2[VEC:2 * VEC] + dot(e2[0:VEC], wlo[...])

        def take_back(first, which):
            arrive(backs, which)
            for q in range(first, first + 4):
                at_q = slice(q * 128, (q + 1) * 128)
                pair = both((rvb if REMOTE else svb)[m, ORDER[q]])
                for th in range(OWN):
                    blhs[th * 2 * VEC:(th + 1) * 2 * VEC, at_q] = pair * jnp.concatenate([smb[th, :, at_q]] * 4, axis=0)
            at_f = slice(first * 128, (first + 4) * 128)
            return dot(blhs[:, at_f], ohb[at_f, :])

        got = take_back(0, CARD)
        for th in range(OWN):
            own[:, th * LO:(th + 1) * LO] += block_of(got, th)
        got = take_back(4, DIAG)
        alpha = jnp.where(m == 0, 1.0 / CHEB_HALF, 2.0 / CHEB_HALF)
        for th in range(OWN):
            at_t = slice(th * LO, (th + 1) * LO)
            new = alpha * (own[:, at_t] + block_of(got, th)) - prev[:, at_t]
            prev[:, at_t] = out[:, at_t]
            out[:, at_t] = new

        @pl.when(m < DEGREES - 1)
        def _():
            field_rows()
            send_values(m + 1, lambda: None)

        sent(backs, coefs)
        return carry

    lax.fori_loop(0, DEGREES, apply, 0)


REMOTE = True


def shards(block, potential, cell_nodes, cell_scale, stiffness, send_nodes, proj_nodes, proj_values, coupling):
    nx, ny = lax.axis_size("mx"), lax.axis_size("my")
    vmem = pl.BlockSpec(memory_space=pltpu.VMEM)
    halo = pltpu.VMEM((DEGREES, 8, VEC, 128), F32)
    slab = pltpu.VMEM((DEGREES, 8, 16, 128), F32)
    sem = pltpu.SemaphoreType.DMA((DEGREES, 8))
    hbm = pl.BlockSpec(memory_space=pltpu.HBM)
    args = (
        block, potential.reshape(NODE // 128, 128), cell_nodes.T, stiffness, send_nodes, proj_nodes,
        proj_values.transpose(0, 2, 1, 3), coupling, cell_scale,
    )
    return pl.pallas_call(
        functools.partial(kernel, nx, ny),
        out_shape=jax.ShapeDtypeStruct((VEC, NODE), F32),
        in_specs=[hbm] * len(args),
        out_specs=vmem,
        scratch_shapes=[pltpu.VMEM(one.shape, one.dtype) for one in args[:-1]] + [
            pltpu.SMEM(cell_scale.shape, F32),
            pltpu.SemaphoreType.DMA((len(args),)),
            pltpu.VMEM((VEC, NODE), F32),
            pltpu.VMEM((VEC, NODE), F32),
            pltpu.VMEM((VEC, SLOTS), F32),
            pltpu.VMEM((OWN * 2 * VEC, LO), BF),
            pltpu.VMEM((GHO * 2 * VEC, LO), BF),
            pltpu.VMEM((CELLS * VEC, 256), BF),
            pltpu.VMEM((2 * VEC, SLOTS), BF),
            pltpu.VMEM(((OWN + GHO) * 2 * VEC, SLOTS), BF),
            pltpu.VMEM((OWN * 2 * VEC, SENDS), BF),
            pltpu.VMEM((VEC, PALL), F32),
            pltpu.VMEM((128, 128), jnp.int32),
            pltpu.VMEM((LO, SLOTS), BF),
            pltpu.VMEM((8, SLOTS), jnp.int32),
            pltpu.VMEM((OWN + GHO, 16, SLOTS), BF),
            pltpu.VMEM((SLOTS, LO), BF),
            pltpu.VMEM((LO, SENDS), BF),
            pltpu.VMEM((8, SENDS), jnp.int32),
            pltpu.VMEM((OWN, 16, SENDS), BF),
            pltpu.VMEM((SENDS, LO), BF),
            pltpu.VMEM((512, NODE), F32),
            pltpu.VMEM((PALL, NODE), BF),
            pltpu.VMEM((PALL, NODE), BF),
            pltpu.VMEM((NODE, 512), BF),
            pltpu.VMEM((NODE, 512), BF),
            pltpu.VMEM((128, 128), F32),
            pltpu.VMEM((256, 256), BF),
            pltpu.VMEM((8, 128), F32),
            pltpu.VMEM((16, 128), F32),
            halo, halo, halo, halo, slab, slab, slab, slab,
            sem, sem, sem, sem, sem, sem, sem, sem,
        ],
        compiler_params=pltpu.CompilerParams(
            collective_id=0, has_side_effects=True, vmem_limit_bytes=48 * 1024 * 1024
        ) if REMOTE else pltpu.CompilerParams(has_side_effects=True, vmem_limit_bytes=48 * 1024 * 1024),
        name="filtered",
    )(*args)


def solution(mesh):
    axes = ("mx", "my")
    placed = (
        P(None, axes), P(axes), P(None, axes), P(axes), P(), P(None, axes),
        P(None, axes, None), P(None, axes, None, None), P(axes, None),
    )
    return jax.shard_map(shards, mesh=mesh, in_specs=placed, out_specs=P(None, axes), check_vma=False)
```

```python
import functools

import jax
import jax.numpy as jnp
from jax import lax
from jax.experimental import pallas as pl
from jax.experimental.pallas import tpu as pltpu
from jax.sharding import PartitionSpec as P

DEGREES = 3
CHEB_CENTER = 5.0
CHEB_HALF = 6.0
MESH = pl.DeviceIdType.MESH
OFFS = ((-1, -1), (-1, 0), (-1, 1), (0, -1), (0, 1), (1, -1), (1, 0), (1, 1))
CARD, DIAG = (1, 6, 3, 4), (0, 2, 5, 7)
ORDER = CARD + DIAG

VEC = 32
NODE = 1280
OWN = 5
GHO = 4
LO = 256
CN = 125
CELLS = 32
SLOTS = CELLS * 128
SENDS = 1024
PRO = 18
PPAD = 24
PK = 2 * PPAD
PALL = 9 * PK
BF = jnp.bfloat16
F32 = jnp.float32


def split(x):
    hi = x.astype(BF)
    return hi, (x - hi.astype(F32)).astype(BF)


def both(x):
    hi, lo = split(x)
    return jnp.concatenate([hi, lo], axis=0)


def dot(a, b):
    return jnp.dot(a, b, preferred_element_type=F32)


def dot_nt(a, b):
    return lax.dot_general(a, b, (((1,), (1,)), ((), ())), preferred_element_type=F32)


def block_of(got, th):
    row = th * 2 * VEC
    return got[row:row + VEC] + got[row + VEC:row + 2 * VEC]


def picked(got, high, first, count, acc):
    for th in range(count):
        one = block_of(got, th)
        acc = one if acc is None else jnp.where(high == first + th, one, acc)
    return acc


def hot_rows(row, iota):
    return jnp.where(iota == (row & (LO - 1)), 1.0, 0.0).astype(BF)


def kernel(
    nx, ny,
    a_block, a_pot, a_cnodes, a_stiff, a_sends, a_pnodes, a_pvals, a_coup, a_cscale,
    out,
    block, pot, cnodes, stiff, sends, pnodes, pvals, coup, cscale, insem,
    prev, own, cellown, flhs, glhs, klhs, prods, slhs, blhs, eall,
    ct, ohg, hi8, mb, ohs, ohsend, shi8, smb, ohb, wf, whi, wlo, twhi, twlo, kf, kmat, crow, cslab,
    sva, rva, svb, rvb, svc, rvc, sve, rve,
    sema, sema_r, semb, semb_r, semc, semc_r, seme, seme_r,
):
    ix = lax.axis_index("mx")
    iy = lax.axis_index("my")

    def at(ox, oy):
        return (lax.rem(ix + ox + nx, nx), lax.rem(iy + oy + ny, ny))

    if REMOTE:
        barrier = pltpu.get_barrier_semaphore()
        for k in ORDER[::-1]:
            pl.semaphore_signal(barrier, inc=1, device_id=at(*OFFS[k]), device_id_type=MESH)

    pairs = (
        (a_sends, sends), (a_block, block), (a_cnodes, cnodes), (a_pnodes, pnodes), (a_pvals, pvals),
        (a_stiff, stiff), (a_coup, coup), (a_cscale, cscale), (a_pot, pot),
    )
    loads = {id(dst): pltpu.make_async_copy(src, dst, insem.at[i]) for i, (src, dst) in enumerate(pairs)}
    for one in loads.values():
        one.start()

    def ready(*refs):
        for ref in refs:
            loads[id(ref)].wait()

    def copies(m, src, dst, send, recv, sign):
        return {
            k: pltpu.make_async_remote_copy(
                src_ref=src.at[m, k], dst_ref=dst.at[m, k], send_sem=send.at[m, k], recv_sem=recv.at[m, k],
                device_id=at(sign * OFFS[k][0], sign * OFFS[k][1]), device_id_type=MESH,
            )
            for k in range(8)
        } if REMOTE else {}

    def start(group, which):
        for k in which:
            if REMOTE:
                group[k].start()

    def arrive(group, which):
        for k in which:
            if REMOTE:
                group[k].wait_recv()

    def sent(*groups):
        for group in groups:
            for one in group.values():
                one.wait_send()

    def send_values(m, before_first):
        ghosts = copies(m, sva, rva, sema, sema_r, 1)
        for j in (2, 3, 0, 1):
            at_j = slice(j * LO, (j + 1) * LO)
            acc = picked(dot(flhs[...], ohsend[:, at_j]), shi8[0:1, at_j], 0, OWN, None)
            sva[m, ORDER[2 * j]] = acc[:, 0:128]
            sva[m, ORDER[2 * j + 1]] = acc[:, 128:256]
            if j == 3:
                before_first()
                start(ghosts, DIAG)
        start(ghosts, CARD)

    def field_rows():
        for th in range(OWN):
            flhs[th * 2 * VEC:(th + 1) * 2 * VEC, :] = both(out[:, th * LO:(th + 1) * LO])

    sub = lax.broadcasted_iota(jnp.int32, (LO, 128), 0)
    ready(sends)
    for q, k in enumerate(ORDER):
        at_q = slice(q * 128, (q + 1) * 128)
        row = sends[k:k + 1, :]
        ohsend[:, at_q] = hot_rows(row, sub)
        shi8[:, at_q] = jnp.broadcast_to(row >> 8, (8, 128))
    ready(block)
    out[...] = block[...]
    field_rows()

    def met():
        if REMOTE:
            pl.semaphore_wait(barrier, 8)

    send_values(0, met)

    ct[...] = jnp.full((128, 128), -1, jnp.int32)
    ready(cnodes)
    ct[0:CELLS, 0:CN] = cnodes[...]
    pos = ct[0:CELLS, :]
    slot = (pos >> 7) - 2 * OWN
    new = slot
    for q, k in enumerate(ORDER):
        new = jnp.where(slot == k, q, new)
    ct[0:CELLS, :] = jnp.where(slot >= 0, ((new + 2 * OWN) << 7) + (pos & 127), pos)
    for q, k in enumerate(ORDER):
        ct[CELLS + q:CELLS + q + 1, :] = sends[k:k + 1, :]
    cols = ct[...].T
    lane = lax.broadcasted_iota(jnp.int32, (128, LO), 1)
    for c in range(CELLS):
        at_c = slice(c * 128, (c + 1) * 128)
        row = ct[c:c + 1, :]
        ohg[:, at_c] = hot_rows(row, sub)
        ohs[at_c, :] = hot_rows(jnp.broadcast_to(cols[:, c:c + 1], (128, LO)), lane)
        high = jnp.broadcast_to(row >> 8, (16, 128))
        hi8[:, at_c] = high[0:8]
        for th in range(OWN + GHO):
            mb[th, :, at_c] = jnp.where(high == th, 1.0, 0.0).astype(BF)
    for q in range(8):
        at_q = slice(q * 128, (q + 1) * 128)
        high = jnp.broadcast_to(ct[CELLS + q:CELLS + q + 1, :] >> 8, (16, 128))
        ohb[at_q, :] = hot_rows(jnp.broadcast_to(cols[:, CELLS + q:CELLS + q + 1], (128, LO)), lane)
        for th in range(OWN):
            smb[th, :, at_q] = jnp.where(high == th, 1.0, 0.0).astype(BF)

    ready(pnodes, pvals)
    sub2 = lax.broadcasted_iota(jnp.int32, (LO, LO), 0)
    pad = jnp.zeros((PPAD - PRO, LO), F32)
    for k in range(9):
        parts = []
        for a in range(2):
            row = pnodes[k, a:a + 1, :]
            high = jnp.broadcast_to(row >> 8, (16, LO))
            v = jnp.concatenate([pvals[k, :, a, :], pad], axis=0)
            vhi = v.astype(BF).astype(F32)
            v2 = jnp.concatenate([vhi, v - vhi], axis=0).astype(BF)
            rows = []
            for th in range(OWN):
                mask = jnp.where(high == th, 1.0, 0.0).astype(BF)
                rows.append(v2 * jnp.concatenate([mask] * 3, axis=0))
            got = dot_nt(jnp.concatenate(rows, axis=0), hot_rows(row, sub2))
            parts.append([got[th * PK:th * PK + PPAD] + got[th * PK + PPAD:(th + 1) * PK] for th in range(OWN)])
        for th in range(OWN):
            at_t = slice(th * LO, (th + 1) * LO)
            w = jnp.concatenate([parts[0][th], parts[1][th]], axis=0)
            hi, lo = split(w)
            wf[k * PK:(k + 1) * PK, at_t] = w
            whi[k * PK:(k + 1) * PK, at_t] = hi
            wlo[k * PK:(k + 1) * PK, at_t] = lo
    wf[PALL:512, :] = jnp.zeros((512 - PALL, NODE), F32)
    for n in range(NODE // 128):
        at_n = slice(n * 128, (n + 1) * 128)
        for r in range(4):
            at_r = slice(r * 128, (r + 1) * 128)
            hi, lo = split(wf[at_r, at_n].T)
            twhi[at_n, at_r] = hi
            twlo[at_n, at_r] = lo

    ready(stiff, coup, cscale, pot)
    kf[...] = jnp.zeros((128, 128), F32)
    kf[0:CN, 0:CN] = stiff[...]
    khi, klo = split(kf[...])
    for r in range(2):
        kmat[r * 128:(r + 1) * 128, 0:128] = khi
        kmat[r * 128:(r + 1) * 128, 128:256] = klo

    crow[...] = jnp.zeros_like(crow)
    for h in range(2):
        for a in range(2):
            first = 64 * h + PPAD * a
            crow[0:1, first:first + PRO] = coup[a:a + 1, :]
    for m in range(DEGREES):
        for k in range(8):
            svc[m, k] = jnp.zeros((16, 128), F32)
    cslab[...] = jnp.zeros_like(cslab)
    prev[...] = jnp.zeros_like(prev)

    def masked(th, at_c):
        return prods[:, at_c] * jnp.concatenate([mb[th, :, at_c]] * 4, axis=0)

    def scatter_rows(first, count):
        for th in range(first, first + count):
            for c in range(SLOTS // 512):
                at_c = slice(c * 512, (c + 1) * 512)
                slhs[th * 2 * VEC:(th + 1) * 2 * VEC, at_c] = masked(th, at_c)
        return dot(slhs[first * 2 * VEC:(first + count) * 2 * VEC, :], ohs[...])

    def apply(m, carry):
        ghosts = copies(m, sva, rva, sema, sema_r, 1)
        sums = copies(m, svc, rvc, semc, semc_r, 1)
        backs = copies(m, svb, rvb, semb, semb_r, -1)
        coefs = copies(m, sve, rve, seme, seme_r, -1)

        f2 = both(out[...])
        c2 = dot(f2, twhi[...])
        c = c2[0:VEC] + c2[VEC:2 * VEC] + dot(f2[0:VEC], twlo[...])
        for k in range(9):
            piece = c[:, k * PK:(k + 1) * PK]
            if k == 4:
                cslab[:, 0:PK] = piece[0:16]
                cslab[:, 64:64 + PK] = piece[16:32]
            else:
                d = k if k < 4 else k - 1
                svc[m, d, :, 0:PK] = piece[0:16]
                svc[m, d, :, 64:64 + PK] = piece[16:32]
        start(sums, ORDER[::-1])

        for j in range(SLOTS // LO):
            at_j = slice(j * LO, (j + 1) * LO)
            acc = picked(dot(flhs[...], ohg[:, at_j]), hi8[0:1, at_j], 0, OWN, None)
            cellown[:, at_j] = jnp.where(hi8[0:1, at_j] >= 0, acc, 0.0)

        def ghost_columns(first, which, use):
            arrive(ghosts, which)
            for t in range(first, first + 2):
                glhs[t * 2 * VEC:(t + 1) * 2 * VEC, 0:128] = both((rva if REMOTE else sva)[m, ORDER[2 * t]])
                glhs[t * 2 * VEC:(t + 1) * 2 * VEC, 128:256] = both((rva if REMOTE else sva)[m, ORDER[2 * t + 1]])
            part = glhs[first * 2 * VEC:(first + 2) * 2 * VEC, :]
            for j in range(SLOTS // LO):
                at_j = slice(j * LO, (j + 1) * LO)
                use(j, at_j, picked(dot(part, ohg[:, at_j]), hi8[0:1, at_j], OWN + first, 2, cellown[:, at_j]))

        def keep(j, at_j, acc):
            cellown[:, at_j] = acc

        def stack(j, at_j, acc):
            hi, lo = split(acc)
            for h in range(2):
                rows = slice((2 * j + h) * VEC, (2 * j + h + 1) * VEC)
                klhs[rows, 0:128] = hi[:, h * 128:(h + 1) * 128]
                klhs[rows, 128:256] = lo[:, h * 128:(h + 1) * 128]

        ghost_columns(0, CARD, keep)
        ghost_columns(2, DIAG, stack)

        for j in range(CELLS // 8):
            got = dot(klhs[j * 256:(j + 1) * 256, :], kmat[...])
            prod = got[:, 0:128] + got[:, 128:256]
            for i in range(8):
                c0 = j * 8 + i
                prods[:, c0 * 128:(c0 + 1) * 128] = both(prod[i * VEC:(i + 1) * VEC] * cscale[c0])

        arrive(sums, ORDER)
        total = cslab[...]
        for k in range(8):
            total = total + (rvc if REMOTE else svc)[m, k]
        coef = total * crow[0:1, :]
        for k in range(8):
            sve[m, k] = coef
        start(coefs, ORDER[::-1])

        def give_back(first, which):
            got = scatter_rows(OWN + first, 2)
            for t in range(2):
                one = block_of(got, t)
                svb[m, ORDER[2 * (first + t)]] = one[:, 0:128]
                svb[m, ORDER[2 * (first + t) + 1]] = one[:, 128:256]
            start(backs, which)

        give_back(2, DIAG)
        give_back(0, CARD)

        got = scatter_rows(0, OWN)
        for n in range(NODE // 128):
            at_n = slice(n * 128, (n + 1) * 128)
            own[:, at_n] = (pot[n:n + 1, :] - CHEB_CENTER) * out[:, at_n]
        for th in range(OWN):
            own[:, th * LO:(th + 1) * LO] += block_of(got, th)
        sent(ghosts, sums)
        arrive(coefs, ORDER)
        for k in range(9):
            slab = coef if k == 4 else (rve if REMOTE else sve)[m, k if k < 4 else k - 1]
            eall[0:16, k * PK:(k + 1) * PK] = slab[:, 0:PK]
            eall[16:32, k * PK:(k + 1) * PK] = slab[:, 64:64 + PK]
        e2 = both(eall[...])
        s2 = dot(e2, whi[...])
        own[...] += s2[0:VEC] + s2[VEC:2 * VEC] + dot(e2[0:VEC], wlo[...])

        def take_back(first, which):
            arrive(backs, which)
            for q in range(first, first + 4):
                at_q = slice(q * 128, (q + 1) * 128)
                pair = both((rvb if REMOTE else svb)[m, ORDER[q]])
                for th in range(OWN):
                    blhs[th * 2 * VEC:(th + 1) * 2 * VEC, at_q] = pair * jnp.concatenate([smb[th, :, at_q]] * 4, axis=0)
            at_f = slice(first * 128, (first + 4) * 128)
            return dot(blhs[:, at_f], ohb[at_f, :])

        got = take_back(0, CARD)
        for th in range(OWN):
            own[:, th * LO:(th + 1) * LO] += block_of(got, th)
        got = take_back(4, DIAG)
        alpha = jnp.where(m == 0, 1.0 / CHEB_HALF, 2.0 / CHEB_HALF)
        for th in range(OWN):
            at_t = slice(th * LO, (th + 1) * LO)
            new = alpha * (own[:, at_t] + block_of(got, th)) - prev[:, at_t]
            prev[:, at_t] = out[:, at_t]
            out[:, at_t] = new

        @pl.when(m < DEGREES - 1)
        def _():
            field_rows()
            send_values(m + 1, lambda: None)

        sent(backs, coefs)
        return carry

    lax.fori_loop(0, DEGREES, apply, 0)


REMOTE = True


def shards(block, potential, cell_nodes, cell_scale, stiffness, send_nodes, proj_nodes, proj_values, coupling):
    nx, ny = lax.axis_size("mx"), lax.axis_size("my")
    vmem = pl.BlockSpec(memory_space=pltpu.VMEM)
    halo = pltpu.VMEM((DEGREES, 8, VEC, 128), F32)
    slab = pltpu.VMEM((DEGREES, 8, 16, 128), F32)
    sem = pltpu.SemaphoreType.DMA((DEGREES, 8))
    hbm = pl.BlockSpec(memory_space=pltpu.HBM)
    args = (
        block, potential.reshape(NODE // 128, 128), cell_nodes.T, stiffness, send_nodes, proj_nodes,
        proj_values.transpose(0, 2, 1, 3), coupling, cell_scale,
    )
    return pl.pallas_call(
        functools.partial(kernel, nx, ny),
        out_shape=jax.ShapeDtypeStruct((VEC, NODE), F32),
        in_specs=[hbm] * len(args),
        out_specs=vmem,
        scratch_shapes=[pltpu.VMEM(one.shape, one.dtype) for one in args[:-1]] + [
            pltpu.SMEM(cell_scale.shape, F32),
            pltpu.SemaphoreType.DMA((len(args),)),
            pltpu.VMEM((VEC, NODE), F32),
            pltpu.VMEM((VEC, NODE), F32),
            pltpu.VMEM((VEC, SLOTS), F32),
            pltpu.VMEM((OWN * 2 * VEC, LO), BF),
            pltpu.VMEM((GHO * 2 * VEC, LO), BF),
            pltpu.VMEM((CELLS * VEC, 256), BF),
            pltpu.VMEM((2 * VEC, SLOTS), BF),
            pltpu.VMEM(((OWN + GHO) * 2 * VEC, SLOTS), BF),
            pltpu.VMEM((OWN * 2 * VEC, SENDS), BF),
            pltpu.VMEM((VEC, PALL), F32),
            pltpu.VMEM((128, 128), jnp.int32),
            pltpu.VMEM((LO, SLOTS), BF),
            pltpu.VMEM((8, SLOTS), jnp.int32),
            pltpu.VMEM((OWN + GHO, 16, SLOTS), BF),
            pltpu.VMEM((SLOTS, LO), BF),
            pltpu.VMEM((LO, SENDS), BF),
            pltpu.VMEM((8, SENDS), jnp.int32),
            pltpu.VMEM((OWN, 16, SENDS), BF),
            pltpu.VMEM((SENDS, LO), BF),
            pltpu.VMEM((512, NODE), F32),
            pltpu.VMEM((PALL, NODE), BF),
            pltpu.VMEM((PALL, NODE), BF),
            pltpu.VMEM((NODE, 512), BF),
            pltpu.VMEM((NODE, 512), BF),
            pltpu.VMEM((128, 128), F32),
            pltpu.VMEM((256, 256), BF),
            pltpu.VMEM((8, 128), F32),
            pltpu.VMEM((16, 128), F32),
            halo, halo, halo, halo, slab, slab, slab, slab,
            sem, sem, sem, sem, sem, sem, sem, sem,
        ],
        compiler_params=pltpu.CompilerParams(
            collective_id=0, has_side_effects=True, vmem_limit_bytes=56 * 1024 * 1024
        ) if REMOTE else pltpu.CompilerParams(has_side_effects=True, vmem_limit_bytes=56 * 1024 * 1024),
        name="filtered",
    )(*args)


def solution(mesh):
    axes = ("mx", "my")
    placed = (
        P(None, axes), P(axes), P(None, axes), P(axes), P(), P(None, axes),
        P(None, axes, None), P(None, axes, None, None), P(axes, None),
    )
    return jax.shard_map(shards, mesh=mesh, in_specs=placed, out_specs=P(None, axes), check_vma=False)
```

```python
import functools

import jax
import jax.numpy as jnp
from jax import lax
from jax.experimental import pallas as pl
from jax.experimental.pallas import tpu as pltpu
from jax.sharding import PartitionSpec as P

DEGREES = 3
CHEB_CENTER = 5.0
CHEB_HALF = 6.0
MESH = pl.DeviceIdType.MESH
OFFS = ((-1, -1), (-1, 0), (-1, 1), (0, -1), (0, 1), (1, -1), (1, 0), (1, 1))
CARD, DIAG = (1, 6, 3, 4), (0, 2, 5, 7)
ORDER = CARD + DIAG
NINE = tuple(k if k < 4 else k + 1 for k in ORDER) + (4,)

VEC = 32
NODE = 1280
OWN = 5
GHO = 4
LO = 256
CN = 125
CELLS = 32
SLOTS = CELLS * 128
SENDS = 1024
PRO = 18
PPAD = 24
PK = 2 * PPAD
PALL = 9 * PK
BF = jnp.bfloat16
F32 = jnp.float32


def split(x):
    hi = x.astype(BF)
    return hi, (x - hi.astype(F32)).astype(BF)


def both(x):
    hi, lo = split(x)
    return jnp.concatenate([hi, lo], axis=0)


def dot(a, b):
    return jnp.dot(a, b, preferred_element_type=F32)


def dot_nt(a, b):
    return lax.dot_general(a, b, (((1,), (1,)), ((), ())), preferred_element_type=F32)


def block_of(got, th):
    row = th * 2 * VEC
    return got[row:row + VEC] + got[row + VEC:row + 2 * VEC]


def picked(got, high, first, count, acc):
    for th in range(count):
        one = block_of(got, th)
        acc = one if acc is None else jnp.where(high == first + th, one, acc)
    return acc


def hot_rows(row, iota):
    return jnp.where(iota == (row & (LO - 1)), 1.0, 0.0).astype(BF)


def kernel(
    nx, ny,
    a_block, a_pot, a_cnodes, a_stiff, a_sends, a_pnodes, a_pvals, a_coup, a_cscale,
    out,
    block, pot, cnodes, stiff, sends, pnodes, pvals, coup, cscale, insem,
    prev, own, cellown, flhs, glhs, klhs, prods, slhs, blhs, eall,
    ct, ohg, hi8, mb, ohs, ohsend, shi8, smb, ohb, same, pn, wf, whi, wlo, twhi, twlo, kf, kmat, crow, cslab,
    sva, rva, svb, rvb, svc, rvc, sve, rve, sem_s, sem_r,
):
    ix = lax.axis_index("mx")
    iy = lax.axis_index("my")

    def at(ox, oy):
        return (lax.rem(ix + ox + nx, nx), lax.rem(iy + oy + ny, ny))

    if REMOTE:
        barrier = pltpu.get_barrier_semaphore()
        for k in ORDER[::-1]:
            pl.semaphore_signal(barrier, inc=1, device_id=at(*OFFS[k]), device_id_type=MESH)

    pairs = (
        (a_sends, sends), (a_block, block), (a_cnodes, cnodes), (a_pnodes, pnodes), (a_pvals, pvals),
        (a_stiff, stiff), (a_coup, coup), (a_cscale, cscale), (a_pot, pot),
    )
    loads = {id(dst): pltpu.make_async_copy(src, dst, insem.at[i]) for i, (src, dst) in enumerate(pairs)}
    for one in loads.values():
        one.start()

    def ready(*refs):
        for ref in refs:
            loads[id(ref)].wait()

    def group(kind, m, first, count):
        src, dst = ((sva, rva), (svb, rvb), (svc, rvc), (sve, rve))[kind]
        sign = (1, -1, 1, -1)[kind]
        sem = 2 * kind + first // 4

        def copy(where, q):
            return pltpu.make_async_remote_copy(
                src_ref=src.at[m, where], dst_ref=dst.at[m, where], send_sem=sem_s.at[sem], recv_sem=sem_r.at[sem],
                device_id=at(sign * OFFS[ORDER[q]][0], sign * OFFS[ORDER[q]][1]), device_id_type=MESH,
            )

        return copy, first, count

    def start(kind, m, first, count):
        if REMOTE:
            copy, first, count = group(kind, m, first, count)
            for q in reversed(range(first, first + count)):
                copy(q, q).start()

    def arrive(kind, m, first, count):
        if REMOTE:
            copy, first, count = group(kind, m, first, count)
            copy(pl.ds(first, count), first).wait_recv()

    def sent(kind, m, first, count):
        if REMOTE:
            copy, first, count = group(kind, m, first, count)
            copy(pl.ds(first, count), first).wait_send()

    def values_at(m, first):
        for j in range(first // 2, first // 2 + 2):
            at_j = slice(j * LO, (j + 1) * LO)
            acc = picked(dot(flhs[...], ohsend[:, at_j]), shi8[0:1, at_j], 0, OWN, None)
            sva[m, 2 * j] = acc[:, 0:128]
            sva[m, 2 * j + 1] = acc[:, 128:256]

    def projector_sums(m, first):
        f2 = both(out[...])
        if first:
            c2 = dot_nt(f2, whi[...])
            c = c2[0:VEC] + c2[VEC:2 * VEC] + dot_nt(f2[0:VEC], wlo[...])
        else:
            c2 = dot(f2, twhi[...])
            c = c2[0:VEC] + c2[VEC:2 * VEC] + dot(f2[0:VEC], twlo[...])
        for q, k in enumerate(NINE):
            piece = c[:, k * PK:(k + 1) * PK]
            if q == 8:
                cslab[:, 0:PK] = piece[0:16]
                cslab[:, 64:64 + PK] = piece[16:32]
            else:
                svc[m, q, :, 0:PK] = piece[0:16]
                svc[m, q, :, 64:64 + PK] = piece[16:32]
        start(2, m, 0, 8)

    def field_rows(field):
        for th in range(OWN):
            flhs[th * 2 * VEC:(th + 1) * 2 * VEC, :] = both(field[:, th * LO:(th + 1) * LO])

    sub = lax.broadcasted_iota(jnp.int32, (LO, 128), 0)
    ready(sends)
    for q, k in enumerate(ORDER):
        at_q = slice(q * 128, (q + 1) * 128)
        row = sends[k:k + 1, :]
        ohsend[:, at_q] = hot_rows(row, sub)
        shi8[:, at_q] = jnp.broadcast_to(row >> 8, (8, 128))
    ready(block)
    out[...] = block[...]
    field_rows(out)

    values_at(0, 4)
    if REMOTE:
        pl.semaphore_wait(barrier, 8)
    start(0, 0, 4, 4)
    values_at(0, 0)
    start(0, 0, 0, 4)

    ready(pnodes, pvals)
    pn[...] = jnp.zeros_like(pn)
    for k in range(9):
        pn[2 * k:2 * k + 2, :] = pnodes[k]
    pcols = jnp.concatenate([pn[:, 0:128].T, pn[:, 128:256].T], axis=0)
    lane2 = lax.broadcasted_iota(jnp.int32, (LO, LO), 1)
    pad = jnp.zeros((PPAD - PRO, LO), F32)
    for k in range(9):
        parts = []
        for a in range(2):
            row = pnodes[k, a:a + 1, :]
            high = jnp.broadcast_to(row >> 8, (16, LO))
            v = jnp.concatenate([pvals[k, :, a, :], pad], axis=0)
            vhi = v.astype(BF).astype(F32)
            v2 = jnp.concatenate([vhi, v - vhi], axis=0).astype(BF)
            rows = []
            for th in range(OWN):
                mask = jnp.where(high == th, 1.0, 0.0).astype(BF)
                rows.append(v2 * jnp.concatenate([mask] * 3, axis=0))
            col = jnp.broadcast_to(pcols[:, 2 * k + a:2 * k + a + 1], (LO, LO))
            got = dot(jnp.concatenate(rows, axis=0), hot_rows(col, lane2))
            parts.append([got[th * PK:th * PK + PPAD] + got[th * PK + PPAD:(th + 1) * PK] for th in range(OWN)])
        for th in range(OWN):
            at_t = slice(th * LO, (th + 1) * LO)
            w = jnp.concatenate([parts[0][th], parts[1][th]], axis=0)
            hi, lo = split(w)
            wf[k * PK:(k + 1) * PK, at_t] = w
            whi[k * PK:(k + 1) * PK, at_t] = hi
            wlo[k * PK:(k + 1) * PK, at_t] = lo
    for m in range(DEGREES):
        for k in range(8):
            svc[m, k] = jnp.zeros((16, 128), F32)
    cslab[...] = jnp.zeros_like(cslab)
    projector_sums(0, True)

    ct[...] = jnp.full((128, 128), -1, jnp.int32)
    ready(cnodes)
    ct[0:CELLS, 0:CN] = cnodes[...]
    pos = ct[0:CELLS, :]
    slot = (pos >> 7) - 2 * OWN
    new = slot
    for q, k in enumerate(ORDER):
        new = jnp.where(slot == k, q, new)
    ct[0:CELLS, :] = jnp.where(slot >= 0, ((new + 2 * OWN) << 7) + (pos & 127), pos)
    for q, k in enumerate(ORDER):
        ct[CELLS + q:CELLS + q + 1, :] = sends[k:k + 1, :]
    cols = ct[...].T
    lane = lax.broadcasted_iota(jnp.int32, (128, LO), 1)
    for c in range(CELLS):
        at_c = slice(c * 128, (c + 1) * 128)
        row = ct[c:c + 1, :]
        ohg[:, at_c] = hot_rows(row, sub)
        ohs[at_c, :] = hot_rows(jnp.broadcast_to(cols[:, c:c + 1], (128, LO)), lane)
        high = jnp.broadcast_to(row >> 8, (16, 128))
        hi8[:, at_c] = high[0:8]
        for th in range(OWN + GHO):
            mb[th, :, at_c] = jnp.where(high == th, 1.0, 0.0).astype(BF)
    for q in range(8):
        at_q = slice(q * 128, (q + 1) * 128)
        high = jnp.broadcast_to(ct[CELLS + q:CELLS + q + 1, :] >> 8, (16, 128))
        ohb[at_q, :] = hot_rows(jnp.broadcast_to(cols[:, CELLS + q:CELLS + q + 1], (128, LO)), lane)
        for th in range(OWN):
            smb[th, :, at_q] = jnp.where(high == th, 1.0, 0.0).astype(BF)
    for q in range(4):
        col = jnp.broadcast_to(cols[:, CELLS + 4 + q:CELLS + 5 + q], (128, 128))
        for p in range(4):
            hit = col == ct[CELLS + 4 + p:CELLS + 5 + p, :]
            same[q * 128:(q + 1) * 128, p * 128:(p + 1) * 128] = jnp.where(hit, 1.0, 0.0).astype(BF)

    ready(stiff, coup, cscale, pot)
    kf[...] = jnp.zeros((128, 128), F32)
    kf[0:CN, 0:CN] = stiff[...]
    khi, klo = split(kf[...])
    for r in range(2):
        kmat[r * 128:(r + 1) * 128, 0:128] = khi
        kmat[r * 128:(r + 1) * 128, 128:256] = klo

    crow[...] = jnp.zeros_like(crow)
    for h in range(2):
        for a in range(2):
            first = 64 * h + PPAD * a
            crow[0:1, first:first + PRO] = coup[a:a + 1, :]
    prev[...] = jnp.zeros_like(prev)


    def turned():
        wf[PALL:512, :] = jnp.zeros((512 - PALL, NODE), F32)
        for n in range(NODE // 128):
            at_n = slice(n * 128, (n + 1) * 128)
            for r in range(4):
                at_r = slice(r * 128, (r + 1) * 128)
                hi, lo = split(wf[at_r, at_n].T)
                twhi[at_n, at_r] = hi
                twlo[at_n, at_r] = lo

    def masked_rows(pair, first, count, at_c):
        for th in range(first, first + count):
            slhs[th * 2 * VEC:(th + 1) * 2 * VEC, at_c] = pair * jnp.concatenate([mb[th, :, at_c]] * 4, axis=0)

    def scatter_rows(first, count):
        for c in range(SLOTS // 512):
            at_c = slice(c * 512, (c + 1) * 512)
            masked_rows(prods[:, at_c], first, count, at_c)
        return dot(slhs[first * 2 * VEC:(first + count) * 2 * VEC, :], ohs[...])

    ghosts_in = rva if REMOTE else sva
    replies_in = rvb if REMOTE else svb
    sums_in = rvc if REMOTE else svc
    coefs_in = rve if REMOTE else sve

    def apply(m, carry):
        for j in range(SLOTS // LO):
            at_j = slice(j * LO, (j + 1) * LO)
            acc = picked(dot(flhs[...], ohg[:, at_j]), hi8[0:1, at_j], 0, OWN, None)
            cellown[:, at_j] = jnp.where(hi8[0:1, at_j] >= 0, acc, 0.0)

        def ghost_rows(first):
            arrive(0, m, 2 * first, 4)
            for t in range(first, first + 2):
                glhs[t * 2 * VEC:(t + 1) * 2 * VEC, 0:128] = both(ghosts_in[m, 2 * t])
                glhs[t * 2 * VEC:(t + 1) * 2 * VEC, 128:256] = both(ghosts_in[m, 2 * t + 1])

        def ghost_columns(first, at_j):
            got = dot(glhs[first * 2 * VEC:(first + 2) * 2 * VEC, :], ohg[:, at_j])
            return picked(got, hi8[0:1, at_j], OWN + first, 2, cellown[:, at_j])

        ghost_rows(0)
        for j in range(SLOTS // LO):
            at_j = slice(j * LO, (j + 1) * LO)
            cellown[:, at_j] = ghost_columns(0, at_j)
        sent(0, m, 0, 4)
        sent(2, m, 0, 8)

        ghost_rows(2)
        got = None
        for g in range(4):
            for j in range(4 * g, 4 * g + 4):
                hi, lo = split(ghost_columns(2, slice(j * LO, (j + 1) * LO)))
                for h in range(2):
                    rows = slice((2 * j + h) * VEC, (2 * j + h + 1) * VEC)
                    klhs[rows, 0:128] = hi[:, h * 128:(h + 1) * 128]
                    klhs[rows, 128:256] = lo[:, h * 128:(h + 1) * 128]
            prod2 = dot(klhs[g * 256:(g + 1) * 256, :], kmat[...])
            prod = prod2[:, 0:128] + prod2[:, 128:256]
            for i in range(8):
                c0 = g * 8 + i
                at_c = slice(c0 * 128, (c0 + 1) * 128)
                pair = both(prod[i * VEC:(i + 1) * VEC] * cscale[c0])
                prods[:, at_c] = pair
                masked_rows(pair, OWN + 2, 2, at_c)
            at_g = slice(g * 1024, (g + 1) * 1024)
            some = dot(slhs[(OWN + 2) * 2 * VEC:(OWN + 4) * 2 * VEC, at_g], ohs[at_g, :])
            got = some if got is None else got + some
            if g == 2:
                arrive(2, m, 0, 8)
                total = cslab[...]
                for q in range(8):
                    total = total + sums_in[m, q]
                coef = total * crow[0:1, :]
                for q in range(8):
                    sve[m, q] = coef
                start(3, m, 0, 8)

        def give_back(first, got):
            for t in range(2):
                one = block_of(got, t)
                svb[m, 2 * (first + t)] = one[:, 0:128]
                svb[m, 2 * (first + t) + 1] = one[:, 128:256]
            start(1, m, 2 * first, 4)

        give_back(2, got)
        give_back(0, scatter_rows(OWN, 2))

        got = scatter_rows(0, OWN)
        for n in range(NODE // 128):
            at_n = slice(n * 128, (n + 1) * 128)
            own[:, at_n] = (pot[n:n + 1, :] - CHEB_CENTER) * out[:, at_n]
        for th in range(OWN):
            own[:, th * LO:(th + 1) * LO] += block_of(got, th)
        sent(0, m, 4, 4)

        @pl.when(m == 0)
        def _():
            turned()

        arrive(3, m, 0, 8)
        for q, k in enumerate(NINE):
            slab = coef if q == 8 else coefs_in[m, q]
            eall[0:16, k * PK:(k + 1) * PK] = slab[:, 0:PK]
            eall[16:32, k * PK:(k + 1) * PK] = slab[:, 64:64 + PK]
        e2 = both(eall[...])
        s2 = dot(e2, whi[...])
        own[...] += s2[0:VEC] + s2[VEC:2 * VEC] + dot(e2[0:VEC], wlo[...])

        def reply_rows(first):
            for q in range(first, first + 4):
                at_q = slice(q * 128, (q + 1) * 128)
                pair = both(replies_in[m, q])
                for th in range(OWN):
                    blhs[th * 2 * VEC:(th + 1) * 2 * VEC, at_q] = pair * jnp.concatenate([smb[th, :, at_q]] * 4, axis=0)
            at_f = slice(first * 128, (first + 4) * 128)
            return dot(blhs[:, at_f], ohb[at_f, :])

        alpha = jnp.where(m == 0, 1.0 / CHEB_HALF, 2.0 / CHEB_HALF)
        arrive(1, m, 0, 4)
        got = reply_rows(0)
        for th in range(OWN):
            at_t = slice(th * LO, (th + 1) * LO)
            own[:, at_t] = alpha * (own[:, at_t] + block_of(got, th)) - prev[:, at_t]

        @pl.when(m < DEGREES - 1)
        def _():
            field_rows(own)
            values_at(m + 1, 4)

        arrive(1, m, 4, 4)

        @pl.when(m < DEGREES - 1)
        def _():
            pair = jnp.concatenate([both(replies_in[m, q]) for q in range(4, 8)], axis=1)
            got = dot(pair, same[...])
            more = alpha * (got[0:VEC] + got[VEC:2 * VEC])
            for q in range(4):
                sva[m + 1, 4 + q] += more[:, q * 128:(q + 1) * 128]
            start(0, m + 1, 4, 4)

        got = reply_rows(4)
        for th in range(OWN):
            at_t = slice(th * LO, (th + 1) * LO)
            new = own[:, at_t] + alpha * block_of(got, th)
            prev[:, at_t] = out[:, at_t]
            out[:, at_t] = new

        @pl.when(m < DEGREES - 1)
        def _():
            field_rows(out)
            values_at(m + 1, 0)
            start(0, m + 1, 0, 4)
            projector_sums(m + 1, False)

        sent(1, m, 0, 4)
        sent(1, m, 4, 4)
        sent(3, m, 0, 8)
        return carry

    lax.fori_loop(0, DEGREES, apply, 0)


REMOTE = True


def shards(block, potential, cell_nodes, cell_scale, stiffness, send_nodes, proj_nodes, proj_values, coupling):
    nx, ny = lax.axis_size("mx"), lax.axis_size("my")
    vmem = pl.BlockSpec(memory_space=pltpu.VMEM)
    halo = pltpu.VMEM((DEGREES, 8, VEC, 128), F32)
    slab = pltpu.VMEM((DEGREES, 8, 16, 128), F32)
    sem = pltpu.SemaphoreType.DMA((8,))
    hbm = pl.BlockSpec(memory_space=pltpu.HBM)
    args = (
        block, potential.reshape(NODE // 128, 128), cell_nodes.T, stiffness, send_nodes, proj_nodes,
        proj_values.transpose(0, 2, 1, 3), coupling, cell_scale,
    )
    args = tuple(pltpu.with_memory_space_constraint(one, pltpu.HBM) for one in args)
    return pl.pallas_call(
        functools.partial(kernel, nx, ny),
        out_shape=jax.ShapeDtypeStruct((VEC, NODE), F32),
        in_specs=[hbm] * len(args),
        out_specs=vmem,
        scratch_shapes=[pltpu.VMEM(one.shape, one.dtype) for one in args[:-1]] + [
            pltpu.SMEM(cell_scale.shape, F32),
            pltpu.SemaphoreType.DMA((len(args),)),
            pltpu.VMEM((VEC, NODE), F32),
            pltpu.VMEM((VEC, NODE), F32),
            pltpu.VMEM((VEC, SLOTS), F32),
            pltpu.VMEM((OWN * 2 * VEC, LO), BF),
            pltpu.VMEM((GHO * 2 * VEC, LO), BF),
            pltpu.VMEM((CELLS * VEC, 256), BF),
            pltpu.VMEM((2 * VEC, SLOTS), BF),
            pltpu.VMEM(((OWN + GHO) * 2 * VEC, SLOTS), BF),
            pltpu.VMEM((OWN * 2 * VEC, SENDS), BF),
            pltpu.VMEM((VEC, PALL), F32),
            pltpu.VMEM((128, 128), jnp.int32),
            pltpu.VMEM((LO, SLOTS), BF),
            pltpu.VMEM((8, SLOTS), jnp.int32),
            pltpu.VMEM((OWN + GHO, 16, SLOTS), BF),
            pltpu.VMEM((SLOTS, LO), BF),
            pltpu.VMEM((LO, SENDS), BF),
            pltpu.VMEM((8, SENDS), jnp.int32),
            pltpu.VMEM((OWN, 16, SENDS), BF),
            pltpu.VMEM((SENDS, LO), BF),
            pltpu.VMEM((512, 512), BF),
            pltpu.VMEM((128, LO), jnp.int32),
            pltpu.VMEM((512, NODE), F32),
            pltpu.VMEM((PALL, NODE), BF),
            pltpu.VMEM((PALL, NODE), BF),
            pltpu.VMEM((NODE, 512), BF),
            pltpu.VMEM((NODE, 512), BF),
            pltpu.VMEM((128, 128), F32),
            pltpu.VMEM((256, 256), BF),
            pltpu.VMEM((8, 128), F32),
            pltpu.VMEM((16, 128), F32),
            halo, halo, halo, halo, slab, slab, slab, slab,
            sem, sem,
        ],
        compiler_params=pltpu.CompilerParams(
            collective_id=0, has_side_effects=True, vmem_limit_bytes=48 * 1024 * 1024
        ) if REMOTE else pltpu.CompilerParams(has_side_effects=True, vmem_limit_bytes=48 * 1024 * 1024),
        name="filtered",
    )(*args)


def solution(mesh):
    axes = ("mx", "my")
    placed = (
        P(None, axes), P(axes), P(None, axes), P(axes), P(), P(None, axes),
        P(None, axes, None), P(None, axes, None, None), P(axes, None),
    )
    return jax.shard_map(shards, mesh=mesh, in_specs=placed, out_specs=P(None, axes), check_vma=False)
```

```python
import functools

import jax
import jax.numpy as jnp
from jax import lax
from jax.experimental import pallas as pl
from jax.experimental.pallas import tpu as pltpu
from jax.sharding import PartitionSpec as P

DEGREES = 3
CHEB_CENTER = 5.0
CHEB_HALF = 6.0
MESH = pl.DeviceIdType.MESH
OFFS = ((-1, -1), (-1, 0), (-1, 1), (0, -1), (0, 1), (1, -1), (1, 0), (1, 1))
CARD, DIAG = (1, 6, 3, 4), (0, 2, 5, 7)
ORDER = CARD + DIAG
NINE = tuple(k if k < 4 else k + 1 for k in ORDER) + (4,)

VEC = 32
NODE = 1280
OWN = 5
GHO = 4
LO = 256
CN = 125
CELLS = 32
SLOTS = CELLS * 128
SENDS = 1024
PRO = 18
PPAD = 24
PK = 2 * PPAD
PALL = 9 * PK
BF = jnp.bfloat16
F32 = jnp.float32


def split(x):
    hi = x.astype(BF)
    return hi, (x - hi.astype(F32)).astype(BF)


def both(x):
    hi, lo = split(x)
    return jnp.concatenate([hi, lo], axis=0)


def dot(a, b):
    return jnp.dot(a, b, preferred_element_type=F32)


def dot_nt(a, b):
    return lax.dot_general(a, b, (((1,), (1,)), ((), ())), preferred_element_type=F32)


def block_of(got, th):
    row = th * 2 * VEC
    return got[row:row + VEC] + got[row + VEC:row + 2 * VEC]


def picked(got, high, first, count, acc):
    for th in range(count):
        one = block_of(got, th)
        acc = one if acc is None else jnp.where(high == first + th, one, acc)
    return acc


def hot_rows(row, iota):
    return jnp.where(iota == (row & (LO - 1)), 1.0, 0.0).astype(BF)


def kernel(
    nx, ny,
    a_block, a_pot, a_cnodes, a_stiff, a_sends, a_pnodes, a_pvals, a_coup, a_cscale,
    out,
    block, pot, cnodes, stiff, sends, pnodes, pvals, coup, cscale, insem,
    prev, own, cellown, flhs, glhs, klhs, prods, slhs, blhs, eall,
    ct, ohg, hi8, mb, ohs, ohsend, shi8, smb, ohb, same, pn, wf, whi, wlo, twhi, twlo, kf, kmat, crow, cslab,
    sva, rva, svb, rvb, svc, rvc, sve, rve, sem_s, sem_r,
):
    ix = lax.axis_index("mx")
    iy = lax.axis_index("my")

    def at(ox, oy):
        return (lax.rem(ix + ox + nx, nx), lax.rem(iy + oy + ny, ny))

    if REMOTE:
        barrier = pltpu.get_barrier_semaphore()
        for k in ORDER[::-1]:
            pl.semaphore_signal(barrier, inc=1, device_id=at(*OFFS[k]), device_id_type=MESH)

    pairs = (
        (a_sends, sends), (a_block, block), (a_cnodes, cnodes), (a_pnodes, pnodes), (a_pvals, pvals),
        (a_stiff, stiff), (a_coup, coup), (a_cscale, cscale), (a_pot, pot),
    )
    loads = {id(dst): pltpu.make_async_copy(src, dst, insem.at[i]) for i, (src, dst) in enumerate(pairs)}
    for one in loads.values():
        one.start()

    def ready(*refs):
        for ref in refs:
            loads[id(ref)].wait()

    def group(kind, m, first, count):
        src, dst = ((sva, rva), (svb, rvb), (svc, rvc), (sve, rve))[kind]
        sign = (1, -1, 1, -1)[kind]
        sem = 2 * kind + first // 4

        def copy(where, q):
            return pltpu.make_async_remote_copy(
                src_ref=src.at[m, where], dst_ref=dst.at[m, where], send_sem=sem_s.at[sem], recv_sem=sem_r.at[sem],
                device_id=at(sign * OFFS[ORDER[q]][0], sign * OFFS[ORDER[q]][1]), device_id_type=MESH,
            )

        return copy, first, count

    def start(kind, m, first, count):
        if REMOTE:
            copy, first, count = group(kind, m, first, count)
            for q in reversed(range(first, first + count)):
                copy(q, q).start()

    def arrive(kind, m, first, count):
        if REMOTE:
            copy, first, count = group(kind, m, first, count)
            copy(pl.ds(first, count), first).wait_recv()

    def sent(kind, m, first, count):
        if REMOTE:
            copy, first, count = group(kind, m, first, count)
            copy(pl.ds(first, count), first).wait_send()

    def values_at(m, first):
        for j in range(first // 2, first // 2 + 2):
            at_j = slice(j * LO, (j + 1) * LO)
            acc = picked(dot(flhs[...], ohsend[:, at_j]), shi8[0:1, at_j], 0, OWN, None)
            sva[m, 2 * j] = acc[:, 0:128]
            sva[m, 2 * j + 1] = acc[:, 128:256]

    def projector_sums(m, first):
        f2 = both(out[...])
        if first:
            c2 = dot_nt(f2, whi[...])
            c = c2[0:VEC] + c2[VEC:2 * VEC] + dot_nt(f2[0:VEC], wlo[...])
        else:
            c2 = dot(f2, twhi[...])
            c = c2[0:VEC] + c2[VEC:2 * VEC] + dot(f2[0:VEC], twlo[...])
        for q, k in enumerate(NINE):
            piece = c[:, k * PK:(k + 1) * PK]
            if q == 8:
                cslab[:, 0:PK] = piece[0:16]
                cslab[:, 64:64 + PK] = piece[16:32]
            else:
                svc[m, q, :, 0:PK] = piece[0:16]
                svc[m, q, :, 64:64 + PK] = piece[16:32]
        start(2, m, 0, 8)

    def field_rows(field):
        for th in range(OWN):
            flhs[th * 2 * VEC:(th + 1) * 2 * VEC, :] = both(field[:, th * LO:(th + 1) * LO])

    sub = lax.broadcasted_iota(jnp.int32, (LO, 128), 0)
    ready(sends)
    for q, k in enumerate(ORDER):
        at_q = slice(q * 128, (q + 1) * 128)
        row = sends[k:k + 1, :]
        ohsend[:, at_q] = hot_rows(row, sub)
        shi8[:, at_q] = jnp.broadcast_to(row >> 8, (8, 128))
    ready(block)
    out[...] = block[...]
    field_rows(out)

    values_at(0, 4)
    values_at(0, 0)

    ready(pnodes, pvals)
    pn[...] = jnp.zeros_like(pn)
    for k in range(9):
        pn[2 * k:2 * k + 2, :] = pnodes[k]
    pcols = jnp.concatenate([pn[:, 0:128].T, pn[:, 128:256].T], axis=0)
    lane2 = lax.broadcasted_iota(jnp.int32, (LO, LO), 1)
    pad = jnp.zeros((PPAD - PRO, LO), F32)
    for k in range(9):
        parts = []
        for a in range(2):
            row = pnodes[k, a:a + 1, :]
            high = jnp.broadcast_to(row >> 8, (16, LO))
            v = jnp.concatenate([pvals[k, :, a, :], pad], axis=0)
            vhi = v.astype(BF).astype(F32)
            v2 = jnp.concatenate([vhi, v - vhi], axis=0).astype(BF)
            rows = []
            for th in range(OWN):
                mask = jnp.where(high == th, 1.0, 0.0).astype(BF)
                rows.append(v2 * jnp.concatenate([mask] * 3, axis=0))
            col = jnp.broadcast_to(pcols[:, 2 * k + a:2 * k + a + 1], (LO, LO))
            got = dot(jnp.concatenate(rows, axis=0), hot_rows(col, lane2))
            parts.append([got[th * PK:th * PK + PPAD] + got[th * PK + PPAD:(th + 1) * PK] for th in range(OWN)])
        for th in range(OWN):
            at_t = slice(th * LO, (th + 1) * LO)
            w = jnp.concatenate([parts[0][th], parts[1][th]], axis=0)
            hi, lo = split(w)
            wf[k * PK:(k + 1) * PK, at_t] = w
            whi[k * PK:(k + 1) * PK, at_t] = hi
            wlo[k * PK:(k + 1) * PK, at_t] = lo
    for m in range(DEGREES):
        for k in range(8):
            svc[m, k] = jnp.zeros((16, 128), F32)
    cslab[...] = jnp.zeros_like(cslab)
    if REMOTE:
        pl.semaphore_wait(barrier, 8)
    start(0, 0, 4, 4)
    start(0, 0, 0, 4)
    projector_sums(0, True)

    ct[...] = jnp.full((128, 128), -1, jnp.int32)
    ready(cnodes)
    ct[0:CELLS, 0:CN] = cnodes[...]
    pos = ct[0:CELLS, :]
    slot = (pos >> 7) - 2 * OWN
    new = slot
    for q, k in enumerate(ORDER):
        new = jnp.where(slot == k, q, new)
    ct[0:CELLS, :] = jnp.where(slot >= 0, ((new + 2 * OWN) << 7) + (pos & 127), pos)
    for q, k in enumerate(ORDER):
        ct[CELLS + q:CELLS + q + 1, :] = sends[k:k + 1, :]
    cols = ct[...].T
    lane = lax.broadcasted_iota(jnp.int32, (128, LO), 1)
    for c in range(CELLS):
        at_c = slice(c * 128, (c + 1) * 128)
        row = ct[c:c + 1, :]
        ohg[:, at_c] = hot_rows(row, sub)
        ohs[at_c, :] = hot_rows(jnp.broadcast_to(cols[:, c:c + 1], (128, LO)), lane)
        high = jnp.broadcast_to(row >> 8, (16, 128))
        hi8[:, at_c] = high[0:8]
        for th in range(OWN + GHO):
            mb[th, :, at_c] = jnp.where(high == th, 1.0, 0.0).astype(BF)
    for q in range(8):
        at_q = slice(q * 128, (q + 1) * 128)
        high = jnp.broadcast_to(ct[CELLS + q:CELLS + q + 1, :] >> 8, (16, 128))
        ohb[at_q, :] = hot_rows(jnp.broadcast_to(cols[:, CELLS + q:CELLS + q + 1], (128, LO)), lane)
        for th in range(OWN):
            smb[th, :, at_q] = jnp.where(high == th, 1.0, 0.0).astype(BF)
    for q in range(4):
        col = jnp.broadcast_to(cols[:, CELLS + 4 + q:CELLS + 5 + q], (128, 128))
        for p in range(4):
            hit = col == ct[CELLS + 4 + p:CELLS + 5 + p, :]
            same[q * 128:(q + 1) * 128, p * 128:(p + 1) * 128] = jnp.where(hit, 1.0, 0.0).astype(BF)

    ready(stiff, coup, cscale, pot)
    kf[...] = jnp.zeros((128, 128), F32)
    kf[0:CN, 0:CN] = stiff[...]
    khi, klo = split(kf[...])
    for r in range(2):
        kmat[r * 128:(r + 1) * 128, 0:128] = khi
        kmat[r * 128:(r + 1) * 128, 128:256] = klo

    crow[...] = jnp.zeros_like(crow)
    for h in range(2):
        for a in range(2):
            first = 64 * h + PPAD * a
            crow[0:1, first:first + PRO] = coup[a:a + 1, :]
    prev[...] = jnp.zeros_like(prev)


    def turned():
        wf[PALL:512, :] = jnp.zeros((512 - PALL, NODE), F32)
        for n in range(NODE // 128):
            at_n = slice(n * 128, (n + 1) * 128)
            for r in range(4):
                at_r = slice(r * 128, (r + 1) * 128)
                hi, lo = split(wf[at_r, at_n].T)
                twhi[at_n, at_r] = hi
                twlo[at_n, at_r] = lo

    def masked_rows(pair, first, count, at_c):
        for th in range(first, first + count):
            slhs[th * 2 * VEC:(th + 1) * 2 * VEC, at_c] = pair * jnp.concatenate([mb[th, :, at_c]] * 4, axis=0)

    def scatter_rows(first, count):
        for c in range(SLOTS // 512):
            at_c = slice(c * 512, (c + 1) * 512)
            masked_rows(prods[:, at_c], first, count, at_c)
        return dot(slhs[first * 2 * VEC:(first + count) * 2 * VEC, :], ohs[...])

    ghosts_in = rva if REMOTE else sva
    replies_in = rvb if REMOTE else svb
    sums_in = rvc if REMOTE else svc
    coefs_in = rve if REMOTE else sve

    def apply(m, carry):
        for j in range(SLOTS // LO):
            at_j = slice(j * LO, (j + 1) * LO)
            acc = picked(dot(flhs[...], ohg[:, at_j]), hi8[0:1, at_j], 0, OWN, None)
            cellown[:, at_j] = jnp.where(hi8[0:1, at_j] >= 0, acc, 0.0)

        def ghost_rows(first):
            arrive(0, m, 2 * first, 4)
            for t in range(first, first + 2):
                glhs[t * 2 * VEC:(t + 1) * 2 * VEC, 0:128] = both(ghosts_in[m, 2 * t])
                glhs[t * 2 * VEC:(t + 1) * 2 * VEC, 128:256] = both(ghosts_in[m, 2 * t + 1])

        def ghost_columns(first, at_j):
            got = dot(glhs[first * 2 * VEC:(first + 2) * 2 * VEC, :], ohg[:, at_j])
            return picked(got, hi8[0:1, at_j], OWN + first, 2, cellown[:, at_j])

        ghost_rows(0)
        for j in range(SLOTS // LO):
            at_j = slice(j * LO, (j + 1) * LO)
            cellown[:, at_j] = ghost_columns(0, at_j)
        sent(0, m, 0, 4)
        sent(2, m, 0, 8)

        ghost_rows(2)
        got = None
        for g in range(4):
            for j in range(4 * g, 4 * g + 4):
                hi, lo = split(ghost_columns(2, slice(j * LO, (j + 1) * LO)))
                for h in range(2):
                    rows = slice((2 * j + h) * VEC, (2 * j + h + 1) * VEC)
                    klhs[rows, 0:128] = hi[:, h * 128:(h + 1) * 128]
                    klhs[rows, 128:256] = lo[:, h * 128:(h + 1) * 128]
            prod2 = dot(klhs[g * 256:(g + 1) * 256, :], kmat[...])
            prod = prod2[:, 0:128] + prod2[:, 128:256]
            for i in range(8):
                c0 = g * 8 + i
                at_c = slice(c0 * 128, (c0 + 1) * 128)
                pair = both(prod[i * VEC:(i + 1) * VEC] * cscale[c0])
                prods[:, at_c] = pair
                masked_rows(pair, OWN + 2, 2, at_c)
            at_g = slice(g * 1024, (g + 1) * 1024)
            some = dot(slhs[(OWN + 2) * 2 * VEC:(OWN + 4) * 2 * VEC, at_g], ohs[at_g, :])
            got = some if got is None else got + some
            if g == 2:
                arrive(2, m, 0, 8)
                total = cslab[...]
                for q in range(8):
                    total = total + sums_in[m, q]
                coef = total * crow[0:1, :]
                for q in range(8):
                    sve[m, q] = coef
                start(3, m, 0, 8)

        def give_back(first, got):
            for t in range(2):
                one = block_of(got, t)
                svb[m, 2 * (first + t)] = one[:, 0:128]
                svb[m, 2 * (first + t) + 1] = one[:, 128:256]
            start(1, m, 2 * first, 4)

        give_back(2, got)
        give_back(0, scatter_rows(OWN, 2))

        got = scatter_rows(0, OWN)
        for n in range(NODE // 128):
            at_n = slice(n * 128, (n + 1) * 128)
            own[:, at_n] = (pot[n:n + 1, :] - CHEB_CENTER) * out[:, at_n]
        for th in range(OWN):
            own[:, th * LO:(th + 1) * LO] += block_of(got, th)
        sent(0, m, 4, 4)

        @pl.when(m == 0)
        def _():
            turned()

        arrive(3, m, 0, 8)
        for q, k in enumerate(NINE):
            slab = coef if q == 8 else coefs_in[m, q]
            eall[0:16, k * PK:(k + 1) * PK] = slab[:, 0:PK]
            eall[16:32, k * PK:(k + 1) * PK] = slab[:, 64:64 + PK]
        e2 = both(eall[...])
        s2 = dot(e2, whi[...])
        own[...] += s2[0:VEC] + s2[VEC:2 * VEC] + dot(e2[0:VEC], wlo[...])

        def reply_rows(first):
            for q in range(first, first + 4):
                at_q = slice(q * 128, (q + 1) * 128)
                pair = both(replies_in[m, q])
                for th in range(OWN):
                    blhs[th * 2 * VEC:(th + 1) * 2 * VEC, at_q] = pair * jnp.concatenate([smb[th, :, at_q]] * 4, axis=0)
            at_f = slice(first * 128, (first + 4) * 128)
            return dot(blhs[:, at_f], ohb[at_f, :])

        alpha = jnp.where(m == 0, 1.0 / CHEB_HALF, 2.0 / CHEB_HALF)
        arrive(1, m, 0, 4)
        got = reply_rows(0)
        for th in range(OWN):
            at_t = slice(th * LO, (th + 1) * LO)
            own[:, at_t] = alpha * (own[:, at_t] + block_of(got, th)) - prev[:, at_t]

        @pl.when(m < DEGREES - 1)
        def _():
            field_rows(own)
            values_at(m + 1, 4)

        arrive(1, m, 4, 4)

        @pl.when(m < DEGREES - 1)
        def _():
            pair = jnp.concatenate([both(replies_in[m, q]) for q in range(4, 8)], axis=1)
            got = dot(pair, same[...])
            more = alpha * (got[0:VEC] + got[VEC:2 * VEC])
            for q in range(4):
                sva[m + 1, 4 + q] += more[:, q * 128:(q + 1) * 128]
            start(0, m + 1, 4, 4)

        got = reply_rows(4)
        for th in range(OWN):
            at_t = slice(th * LO, (th + 1) * LO)
            new = own[:, at_t] + alpha * block_of(got, th)
            prev[:, at_t] = out[:, at_t]
            out[:, at_t] = new

        @pl.when(m < DEGREES - 1)
        def _():
            field_rows(out)
            values_at(m + 1, 0)
            start(0, m + 1, 0, 4)
            projector_sums(m + 1, False)

        sent(1, m, 0, 4)
        sent(1, m, 4, 4)
        sent(3, m, 0, 8)
        return carry

    lax.fori_loop(0, DEGREES, apply, 0)


REMOTE = True


def shards(block, potential, cell_nodes, cell_scale, stiffness, send_nodes, proj_nodes, proj_values, coupling):
    nx, ny = lax.axis_size("mx"), lax.axis_size("my")
    vmem = pl.BlockSpec(memory_space=pltpu.VMEM)
    halo = pltpu.VMEM((DEGREES, 8, VEC, 128), F32)
    slab = pltpu.VMEM((DEGREES, 8, 16, 128), F32)
    sem = pltpu.SemaphoreType.DMA((8,))
    hbm = pl.BlockSpec(memory_space=pltpu.HBM)
    args = (
        block, potential.reshape(NODE // 128, 128), cell_nodes.T, stiffness, send_nodes, proj_nodes,
        proj_values.transpose(0, 2, 1, 3), coupling, cell_scale,
    )
    args = tuple(pltpu.with_memory_space_constraint(one, pltpu.HBM) for one in args)
    return pl.pallas_call(
        functools.partial(kernel, nx, ny),
        out_shape=jax.ShapeDtypeStruct((VEC, NODE), F32),
        in_specs=[hbm] * len(args),
        out_specs=vmem,
        scratch_shapes=[pltpu.VMEM(one.shape, one.dtype) for one in args[:-1]] + [
            pltpu.SMEM(cell_scale.shape, F32),
            pltpu.SemaphoreType.DMA((len(args),)),
            pltpu.VMEM((VEC, NODE), F32),
            pltpu.VMEM((VEC, NODE), F32),
            pltpu.VMEM((VEC, SLOTS), F32),
            pltpu.VMEM((OWN * 2 * VEC, LO), BF),
            pltpu.VMEM((GHO * 2 * VEC, LO), BF),
            pltpu.VMEM((CELLS * VEC, 256), BF),
            pltpu.VMEM((2 * VEC, SLOTS), BF),
            pltpu.VMEM(((OWN + GHO) * 2 * VEC, SLOTS), BF),
            pltpu.VMEM((OWN * 2 * VEC, SENDS), BF),
            pltpu.VMEM((VEC, PALL), F32),
            pltpu.VMEM((128, 128), jnp.int32),
            pltpu.VMEM((LO, SLOTS), BF),
            pltpu.VMEM((8, SLOTS), jnp.int32),
            pltpu.VMEM((OWN + GHO, 16, SLOTS), BF),
            pltpu.VMEM((SLOTS, LO), BF),
            pltpu.VMEM((LO, SENDS), BF),
            pltpu.VMEM((8, SENDS), jnp.int32),
            pltpu.VMEM((OWN, 16, SENDS), BF),
            pltpu.VMEM((SENDS, LO), BF),
            pltpu.VMEM((512, 512), BF),
            pltpu.VMEM((128, LO), jnp.int32),
            pltpu.VMEM((512, NODE), F32),
            pltpu.VMEM((PALL, NODE), BF),
            pltpu.VMEM((PALL, NODE), BF),
            pltpu.VMEM((NODE, 512), BF),
            pltpu.VMEM((NODE, 512), BF),
            pltpu.VMEM((128, 128), F32),
            pltpu.VMEM((256, 256), BF),
            pltpu.VMEM((8, 128), F32),
            pltpu.VMEM((16, 128), F32),
            halo, halo, halo, halo, slab, slab, slab, slab,
            sem, sem,
        ],
        compiler_params=pltpu.CompilerParams(
            collective_id=0, has_side_effects=True, vmem_limit_bytes=48 * 1024 * 1024
        ) if REMOTE else pltpu.CompilerParams(has_side_effects=True, vmem_limit_bytes=48 * 1024 * 1024),
        name="filtered",
    )(*args)


def solution(mesh):
    axes = ("mx", "my")
    placed = (
        P(None, axes), P(axes), P(None, axes), P(axes), P(), P(None, axes),
        P(None, axes, None), P(None, axes, None, None), P(axes, None),
    )
    return jax.shard_map(shards, mesh=mesh, in_specs=placed, out_specs=P(None, axes), check_vma=False)
```

```python
import functools

import jax
import jax.numpy as jnp
from jax import lax
from jax.experimental import pallas as pl
from jax.experimental.pallas import tpu as pltpu
from jax.sharding import PartitionSpec as P

DEGREES = 3
CHEB_CENTER = 5.0
CHEB_HALF = 6.0
MESH = pl.DeviceIdType.MESH
OFFS = ((-1, -1), (-1, 0), (-1, 1), (0, -1), (0, 1), (1, -1), (1, 0), (1, 1))
CARD, DIAG = (1, 6, 3, 4), (0, 2, 5, 7)
ORDER = CARD + DIAG
NINE = tuple(k if k < 4 else k + 1 for k in ORDER) + (4,)

VEC = 32
NODE = 1280
OWN = 5
GHO = 4
LO = 256
CN = 125
CELLS = 32
SLOTS = CELLS * 128
SENDS = 1024
PRO = 18
PPAD = 24
PK = 2 * PPAD
PALL = 9 * PK
BF = jnp.bfloat16
F32 = jnp.float32


def split(x):
    hi = x.astype(BF)
    return hi, (x - hi.astype(F32)).astype(BF)


def both(x):
    hi, lo = split(x)
    return jnp.concatenate([hi, lo], axis=0)


def dot(a, b):
    return jnp.dot(a, b, preferred_element_type=F32)


def dot_nt(a, b):
    return lax.dot_general(a, b, (((1,), (1,)), ((), ())), preferred_element_type=F32)


def block_of(got, th):
    row = th * 2 * VEC
    return got[row:row + VEC] + got[row + VEC:row + 2 * VEC]


def picked(got, high, first, count, acc):
    for th in range(count):
        one = block_of(got, th)
        acc = one if acc is None else jnp.where(high == first + th, one, acc)
    return acc


def hot_rows(row, iota):
    return jnp.where(iota == (row & (LO - 1)), 1.0, 0.0).astype(BF)


def kernel(
    nx, ny,
    a_block, a_pot, a_cnodes, a_stiff, a_sends, a_pnodes, a_pvals, a_coup, a_cscale,
    out,
    block, pot, cnodes, stiff, sends, pnodes, pvals, coup, cscale, insem,
    prev, own, cellown, flhs, glhs, klhs, prods, slhs, blhs, eall,
    ct, ohg, hi8, mb, ohs, ohsend, shi8, smb, ohb, same, pn, wf, whi, wlo, twhi, twlo, kf, kmat, crow, cslab,
    sva, rva, svb, rvb, svc, rvc, sve, rve, sem_s, sem_r,
):
    ix = lax.axis_index("mx")
    iy = lax.axis_index("my")

    def at(ox, oy):
        return (lax.rem(ix + ox + nx, nx), lax.rem(iy + oy + ny, ny))

    if REMOTE:
        barrier = pltpu.get_barrier_semaphore()
        for k in ORDER[::-1]:
            pl.semaphore_signal(barrier, inc=1, device_id=at(*OFFS[k]), device_id_type=MESH)

    pairs = (
        (a_sends, sends), (a_block, block), (a_cnodes, cnodes), (a_pnodes, pnodes), (a_pvals, pvals),
        (a_stiff, stiff), (a_coup, coup), (a_cscale, cscale), (a_pot, pot),
    )
    loads = {id(dst): pltpu.make_async_copy(src, dst, insem.at[i]) for i, (src, dst) in enumerate(pairs)}
    for one in loads.values():
        one.start()

    def ready(*refs):
        for ref in refs:
            loads[id(ref)].wait()

    def group(kind, m, first, count):
        src, dst = ((sva, rva), (svb, rvb), (svc, rvc), (sve, rve))[kind]
        sign = (1, -1, 1, -1)[kind]
        sem = 2 * kind + first // 4

        def copy(where, q):
            return pltpu.make_async_remote_copy(
                src_ref=src.at[m, where], dst_ref=dst.at[m, where], send_sem=sem_s.at[sem], recv_sem=sem_r.at[sem],
                device_id=at(sign * OFFS[ORDER[q]][0], sign * OFFS[ORDER[q]][1]), device_id_type=MESH,
            )

        return copy, first, count

    def start(kind, m, first, count):
        if REMOTE:
            copy, first, count = group(kind, m, first, count)
            for q in reversed(range(first, first + count)):
                copy(q, q).start()

    def arrive(kind, m, first, count):
        if REMOTE:
            copy, first, count = group(kind, m, first, count)
            copy(pl.ds(first, count), first).wait_recv()

    def sent(kind, m, first, count):
        if REMOTE:
            copy, first, count = group(kind, m, first, count)
            copy(pl.ds(first, count), first).wait_send()

    def values_at(m, first):
        for j in range(first // 2, first // 2 + 2):
            at_j = slice(j * LO, (j + 1) * LO)
            acc = picked(dot(flhs[...], ohsend[:, at_j]), shi8[0:1, at_j], 0, OWN, None)
            sva[m, 2 * j] = acc[:, 0:128]
            sva[m, 2 * j + 1] = acc[:, 128:256]

    def projector_sums(m, first):
        f2 = both(out[...])
        if first:
            c2 = dot_nt(f2, whi[...])
            c = c2[0:VEC] + c2[VEC:2 * VEC] + dot_nt(f2[0:VEC], wlo[...])
        else:
            c2 = dot(f2, twhi[...])
            c = c2[0:VEC] + c2[VEC:2 * VEC] + dot(f2[0:VEC], twlo[...])
        for q, k in enumerate(NINE):
            piece = c[:, k * PK:(k + 1) * PK]
            if q == 8:
                cslab[:, 0:PK] = piece[0:16]
                cslab[:, 64:64 + PK] = piece[16:32]
            else:
                svc[m, q, :, 0:PK] = piece[0:16]
                svc[m, q, :, 64:64 + PK] = piece[16:32]
        if not first:
            start(2, m, 0, 8)

    def field_rows(field):
        for th in range(OWN):
            flhs[th * 2 * VEC:(th + 1) * 2 * VEC, :] = both(field[:, th * LO:(th + 1) * LO])

    sub = lax.broadcasted_iota(jnp.int32, (LO, 128), 0)
    ready(sends)
    for q, k in enumerate(ORDER):
        at_q = slice(q * 128, (q + 1) * 128)
        row = sends[k:k + 1, :]
        ohsend[:, at_q] = hot_rows(row, sub)
        shi8[:, at_q] = jnp.broadcast_to(row >> 8, (8, 128))
    ready(block)
    out[...] = block[...]
    field_rows(out)

    values_at(0, 4)
    values_at(0, 0)

    ready(pnodes, pvals)
    pn[...] = jnp.zeros_like(pn)
    for k in range(9):
        pn[2 * k:2 * k + 2, :] = pnodes[k]
    pcols = jnp.concatenate([pn[:, 0:128].T, pn[:, 128:256].T], axis=0)
    lane2 = lax.broadcasted_iota(jnp.int32, (LO, LO), 1)
    pad = jnp.zeros((PPAD - PRO, LO), F32)
    for k in range(9):
        parts = []
        for a in range(2):
            row = pnodes[k, a:a + 1, :]
            high = jnp.broadcast_to(row >> 8, (16, LO))
            v = jnp.concatenate([pvals[k, :, a, :], pad], axis=0)
            vhi = v.astype(BF).astype(F32)
            v2 = jnp.concatenate([vhi, v - vhi], axis=0).astype(BF)
            rows = []
            for th in range(OWN):
                mask = jnp.where(high == th, 1.0, 0.0).astype(BF)
                rows.append(v2 * jnp.concatenate([mask] * 3, axis=0))
            col = jnp.broadcast_to(pcols[:, 2 * k + a:2 * k + a + 1], (LO, LO))
            got = dot(jnp.concatenate(rows, axis=0), hot_rows(col, lane2))
            parts.append([got[th * PK:th * PK + PPAD] + got[th * PK + PPAD:(th + 1) * PK] for th in range(OWN)])
        for th in range(OWN):
            at_t = slice(th * LO, (th + 1) * LO)
            w = jnp.concatenate([parts[0][th], parts[1][th]], axis=0)
            hi, lo = split(w)
            wf[k * PK:(k + 1) * PK, at_t] = w
            whi[k * PK:(k + 1) * PK, at_t] = hi
            wlo[k * PK:(k + 1) * PK, at_t] = lo
    for m in range(DEGREES):
        for k in range(8):
            svc[m, k] = jnp.zeros((16, 128), F32)
    cslab[...] = jnp.zeros_like(cslab)
    projector_sums(0, True)
    if REMOTE:
        pl.semaphore_wait(barrier, 8)
    start(0, 0, 4, 4)
    start(0, 0, 0, 4)
    start(2, 0, 0, 8)

    ct[...] = jnp.full((128, 128), -1, jnp.int32)
    ready(cnodes)
    ct[0:CELLS, 0:CN] = cnodes[...]
    pos = ct[0:CELLS, :]
    slot = (pos >> 7) - 2 * OWN
    new = slot
    for q, k in enumerate(ORDER):
        new = jnp.where(slot == k, q, new)
    ct[0:CELLS, :] = jnp.where(slot >= 0, ((new + 2 * OWN) << 7) + (pos & 127), pos)
    for q, k in enumerate(ORDER):
        ct[CELLS + q:CELLS + q + 1, :] = sends[k:k + 1, :]
    cols = ct[...].T
    lane = lax.broadcasted_iota(jnp.int32, (128, LO), 1)
    for c in range(CELLS):
        at_c = slice(c * 128, (c + 1) * 128)
        row = ct[c:c + 1, :]
        ohg[:, at_c] = hot_rows(row, sub)
        ohs[at_c, :] = hot_rows(jnp.broadcast_to(cols[:, c:c + 1], (128, LO)), lane)
        high = jnp.broadcast_to(row >> 8, (16, 128))
        hi8[:, at_c] = high[0:8]
        for th in range(OWN + GHO):
            mb[th, :, at_c] = jnp.where(high == th, 1.0, 0.0).astype(BF)
    for q in range(8):
        at_q = slice(q * 128, (q + 1) * 128)
        high = jnp.broadcast_to(ct[CELLS + q:CELLS + q + 1, :] >> 8, (16, 128))
        ohb[at_q, :] = hot_rows(jnp.broadcast_to(cols[:, CELLS + q:CELLS + q + 1], (128, LO)), lane)
        for th in range(OWN):
            smb[th, :, at_q] = jnp.where(high == th, 1.0, 0.0).astype(BF)
    for q in range(4):
        col = jnp.broadcast_to(cols[:, CELLS + 4 + q:CELLS + 5 + q], (128, 128))
        for p in range(4):
            hit = col == ct[CELLS + 4 + p:CELLS + 5 + p, :]
            same[q * 128:(q + 1) * 128, p * 128:(p + 1) * 128] = jnp.where(hit, 1.0, 0.0).astype(BF)

    ready(stiff, coup, cscale, pot)
    kf[...] = jnp.zeros((128, 128), F32)
    kf[0:CN, 0:CN] = stiff[...]
    khi, klo = split(kf[...])
    for r in range(2):
        kmat[r * 128:(r + 1) * 128, 0:128] = khi
        kmat[r * 128:(r + 1) * 128, 128:256] = klo

    crow[...] = jnp.zeros_like(crow)
    for h in range(2):
        for a in range(2):
            first = 64 * h + PPAD * a
            crow[0:1, first:first + PRO] = coup[a:a + 1, :]
    prev[...] = jnp.zeros_like(prev)


    def turned():
        wf[PALL:512, :] = jnp.zeros((512 - PALL, NODE), F32)
        for n in range(NODE // 128):
            at_n = slice(n * 128, (n + 1) * 128)
            for r in range(4):
                at_r = slice(r * 128, (r + 1) * 128)
                hi, lo = split(wf[at_r, at_n].T)
                twhi[at_n, at_r] = hi
                twlo[at_n, at_r] = lo

    def masked_rows(pair, first, count, at_c):
        for th in range(first, first + count):
            slhs[th * 2 * VEC:(th + 1) * 2 * VEC, at_c] = pair * jnp.concatenate([mb[th, :, at_c]] * 4, axis=0)

    def scatter_rows(first, count):
        for c in range(SLOTS // 512):
            at_c = slice(c * 512, (c + 1) * 512)
            masked_rows(prods[:, at_c], first, count, at_c)
        return dot(slhs[first * 2 * VEC:(first + count) * 2 * VEC, :], ohs[...])

    ghosts_in = rva if REMOTE else sva
    replies_in = rvb if REMOTE else svb
    sums_in = rvc if REMOTE else svc
    coefs_in = rve if REMOTE else sve

    def apply(m, carry):
        for j in range(SLOTS // LO):
            at_j = slice(j * LO, (j + 1) * LO)
            acc = picked(dot(flhs[...], ohg[:, at_j]), hi8[0:1, at_j], 0, OWN, None)
            cellown[:, at_j] = jnp.where(hi8[0:1, at_j] >= 0, acc, 0.0)

        def ghost_rows(first):
            arrive(0, m, 2 * first, 4)
            for t in range(first, first + 2):
                glhs[t * 2 * VEC:(t + 1) * 2 * VEC, 0:128] = both(ghosts_in[m, 2 * t])
                glhs[t * 2 * VEC:(t + 1) * 2 * VEC, 128:256] = both(ghosts_in[m, 2 * t + 1])

        def ghost_columns(first, at_j):
            got = dot(glhs[first * 2 * VEC:(first + 2) * 2 * VEC, :], ohg[:, at_j])
            return picked(got, hi8[0:1, at_j], OWN + first, 2, cellown[:, at_j])

        ghost_rows(0)
        for j in range(SLOTS // LO):
            at_j = slice(j * LO, (j + 1) * LO)
            cellown[:, at_j] = ghost_columns(0, at_j)
        sent(0, m, 0, 4)
        sent(2, m, 0, 8)

        ghost_rows(2)
        got = None
        for g in range(4):
            for j in range(4 * g, 4 * g + 4):
                hi, lo = split(ghost_columns(2, slice(j * LO, (j + 1) * LO)))
                for h in range(2):
                    rows = slice((2 * j + h) * VEC, (2 * j + h + 1) * VEC)
                    klhs[rows, 0:128] = hi[:, h * 128:(h + 1) * 128]
                    klhs[rows, 128:256] = lo[:, h * 128:(h + 1) * 128]
            prod2 = dot(klhs[g * 256:(g + 1) * 256, :], kmat[...])
            prod = prod2[:, 0:128] + prod2[:, 128:256]
            for i in range(8):
                c0 = g * 8 + i
                at_c = slice(c0 * 128, (c0 + 1) * 128)
                pair = both(prod[i * VEC:(i + 1) * VEC] * cscale[c0])
                prods[:, at_c] = pair
                masked_rows(pair, OWN + 2, 2, at_c)
            at_g = slice(g * 1024, (g + 1) * 1024)
            some = dot(slhs[(OWN + 2) * 2 * VEC:(OWN + 4) * 2 * VEC, at_g], ohs[at_g, :])
            got = some if got is None else got + some
            if g == 2:
                arrive(2, m, 0, 8)
                total = cslab[...]
                for q in range(8):
                    total = total + sums_in[m, q]
                coef = total * crow[0:1, :]
                for q in range(8):
                    sve[m, q] = coef
                start(3, m, 0, 8)

        def give_back(first, got):
            for t in range(2):
                one = block_of(got, t)
                svb[m, 2 * (first + t)] = one[:, 0:128]
                svb[m, 2 * (first + t) + 1] = one[:, 128:256]
            start(1, m, 2 * first, 4)

        give_back(2, got)
        give_back(0, scatter_rows(OWN, 2))

        got = scatter_rows(0, OWN)
        for n in range(NODE // 128):
            at_n = slice(n * 128, (n + 1) * 128)
            own[:, at_n] = (pot[n:n + 1, :] - CHEB_CENTER) * out[:, at_n]
        for th in range(OWN):
            own[:, th * LO:(th + 1) * LO] += block_of(got, th)
        sent(0, m, 4, 4)

        @pl.when(m == 0)
        def _():
            turned()

        arrive(3, m, 0, 8)
        for q, k in enumerate(NINE):
            slab = coef if q == 8 else coefs_in[m, q]
            eall[0:16, k * PK:(k + 1) * PK] = slab[:, 0:PK]
            eall[16:32, k * PK:(k + 1) * PK] = slab[:, 64:64 + PK]
        e2 = both(eall[...])
        s2 = dot(e2, whi[...])
        own[...] += s2[0:VEC] + s2[VEC:2 * VEC] + dot(e2[0:VEC], wlo[...])

        def reply_rows(first):
            for q in range(first, first + 4):
                at_q = slice(q * 128, (q + 1) * 128)
                pair = both(replies_in[m, q])
                for th in range(OWN):
                    blhs[th * 2 * VEC:(th + 1) * 2 * VEC, at_q] = pair * jnp.concatenate([smb[th, :, at_q]] * 4, axis=0)
            at_f = slice(first * 128, (first + 4) * 128)
            return dot(blhs[:, at_f], ohb[at_f, :])

        alpha = jnp.where(m == 0, 1.0 / CHEB_HALF, 2.0 / CHEB_HALF)
        arrive(1, m, 0, 4)
        got = reply_rows(0)
        for th in range(OWN):
            at_t = slice(th * LO, (th + 1) * LO)
            own[:, at_t] = alpha * (own[:, at_t] + block_of(got, th)) - prev[:, at_t]

        @pl.when(m < DEGREES - 1)
        def _():
            field_rows(own)
            values_at(m + 1, 4)

        arrive(1, m, 4, 4)

        @pl.when(m < DEGREES - 1)
        def _():
            pair = jnp.concatenate([both(replies_in[m, q]) for q in range(4, 8)], axis=1)
            got = dot(pair, same[...])
            more = alpha * (got[0:VEC] + got[VEC:2 * VEC])
            for q in range(4):
                sva[m + 1, 4 + q] += more[:, q * 128:(q + 1) * 128]
            start(0, m + 1, 4, 4)

        got = reply_rows(4)
        for th in range(OWN):
            at_t = slice(th * LO, (th + 1) * LO)
            new = own[:, at_t] + alpha * block_of(got, th)
            prev[:, at_t] = out[:, at_t]
            out[:, at_t] = new

        @pl.when(m < DEGREES - 1)
        def _():
            field_rows(out)
            values_at(m + 1, 0)
            start(0, m + 1, 0, 4)
            projector_sums(m + 1, False)

        sent(1, m, 0, 4)
        sent(1, m, 4, 4)
        sent(3, m, 0, 8)
        return carry

    lax.fori_loop(0, DEGREES, apply, 0)


REMOTE = True


def shards(block, potential, cell_nodes, cell_scale, stiffness, send_nodes, proj_nodes, proj_values, coupling):
    nx, ny = lax.axis_size("mx"), lax.axis_size("my")
    vmem = pl.BlockSpec(memory_space=pltpu.VMEM)
    halo = pltpu.VMEM((DEGREES, 8, VEC, 128), F32)
    slab = pltpu.VMEM((DEGREES, 8, 16, 128), F32)
    sem = pltpu.SemaphoreType.DMA((8,))
    hbm = pl.BlockSpec(memory_space=pltpu.HBM)
    args = (
        block, potential.reshape(NODE // 128, 128), cell_nodes.T, stiffness, send_nodes, proj_nodes,
        proj_values.transpose(0, 2, 1, 3), coupling, cell_scale,
    )
    args = tuple(pltpu.with_memory_space_constraint(one, pltpu.HBM) for one in args)
    return pl.pallas_call(
        functools.partial(kernel, nx, ny),
        out_shape=jax.ShapeDtypeStruct((VEC, NODE), F32),
        in_specs=[hbm] * len(args),
        out_specs=vmem,
        scratch_shapes=[pltpu.VMEM(one.shape, one.dtype) for one in args[:-1]] + [
            pltpu.SMEM(cell_scale.shape, F32),
            pltpu.SemaphoreType.DMA((len(args),)),
            pltpu.VMEM((VEC, NODE), F32),
            pltpu.VMEM((VEC, NODE), F32),
            pltpu.VMEM((VEC, SLOTS), F32),
            pltpu.VMEM((OWN * 2 * VEC, LO), BF),
            pltpu.VMEM((GHO * 2 * VEC, LO), BF),
            pltpu.VMEM((CELLS * VEC, 256), BF),
            pltpu.VMEM((2 * VEC, SLOTS), BF),
            pltpu.VMEM(((OWN + GHO) * 2 * VEC, SLOTS), BF),
            pltpu.VMEM((OWN * 2 * VEC, SENDS), BF),
            pltpu.VMEM((VEC, PALL), F32),
            pltpu.VMEM((128, 128), jnp.int32),
            pltpu.VMEM((LO, SLOTS), BF),
            pltpu.VMEM((8, SLOTS), jnp.int32),
            pltpu.VMEM((OWN + GHO, 16, SLOTS), BF),
            pltpu.VMEM((SLOTS, LO), BF),
            pltpu.VMEM((LO, SENDS), BF),
            pltpu.VMEM((8, SENDS), jnp.int32),
            pltpu.VMEM((OWN, 16, SENDS), BF),
            pltpu.VMEM((SENDS, LO), BF),
            pltpu.VMEM((512, 512), BF),
            pltpu.VMEM((128, LO), jnp.int32),
            pltpu.VMEM((512, NODE), F32),
            pltpu.VMEM((PALL, NODE), BF),
            pltpu.VMEM((PALL, NODE), BF),
            pltpu.VMEM((NODE, 512), BF),
            pltpu.VMEM((NODE, 512), BF),
            pltpu.VMEM((128, 128), F32),
            pltpu.VMEM((256, 256), BF),
            pltpu.VMEM((8, 128), F32),
            pltpu.VMEM((16, 128), F32),
            halo, halo, halo, halo, slab, slab, slab, slab,
            sem, sem,
        ],
        compiler_params=pltpu.CompilerParams(
            collective_id=0, has_side_effects=True, vmem_limit_bytes=48 * 1024 * 1024
        ) if REMOTE else pltpu.CompilerParams(has_side_effects=True, vmem_limit_bytes=48 * 1024 * 1024),
        name="filtered",
    )(*args)


def solution(mesh):
    axes = ("mx", "my")
    placed = (
        P(None, axes), P(axes), P(None, axes), P(axes), P(), P(None, axes),
        P(None, axes, None), P(None, axes, None, None), P(axes, None),
    )
    return jax.shard_map(shards, mesh=mesh, in_specs=placed, out_specs=P(None, axes), check_vma=False)
```
